512 devices in a mesh: tm: 32 (over z_lo, y, core), space: 16 (over z_hi, x).
Axes of the slice: x: 4, y: 8, z: 8 (z_hi: 4, z_lo: 2; z = z_hi * 2 + z_lo), core: 2. Of those that a mesh axis runs over, the one named last changes fastest.
Arguments:
- starts: float32 [32, 256, 128, 128], P('tm', 'space'), may hold values from -6 to 6
- holes: int32 [256, 128, 128], P('space'), may hold values 0 or 1
- rate: float32 [256, 128, 128], P('space'), may hold values from 0.05 to 50
- zones: int32 [2, 256, 128], P(None, 'space'), may hold values from 0 to 7
- zone_htc: float32 [8], replicated, may hold values from 0.3 to 4
- gas: float32 [32, 8], P('tm'), may hold values from -1 to 2
- hold: float32 [32], P('tm'), may hold values from 0.5 to 1
- duration: float32 [32], P('tm'), may hold values from 0.5 to 1.5
- inv_x: bfloat16 [128, 128], replicated, may hold values from 0 to 1, as said below
- inv_y: bfloat16 [128, 128], replicated, may hold values from 0 to 1, as said below
- inv_z: bfloat16 [256, 256], replicated, may hold values from 0 to 1, as said below
Outputs:
- renewed_starts: float32 [32, 256, 128, 128], P('tm', 'space')
The draws below stay inside these ranges and needn't reach their ends.
Inputs may be any that keep to these rules, and one draw needn't show every extreme that they name: `inv_x`: entries are positive. `inv_y`: entries are positive. `inv_z`: entries are positive.
All inputs are finite; a program needn't handle non-finite values. No bound on the sum of `holes` on one device may be relied on, other than what follows from the above.
Results may differ from the reference program's by a relative error of at most 0.0003.
Values may be sent and summed in bfloat16 or wider, within the bound.
A program may use at most 128 MiB of HBM per device.

```python
import math
import jax
import jax.numpy as jnp
from jax import lax

NX = 128
NY = 128
NZ = 256
ZONES = 8
ITERS = 1
PERIOD_INTERVALS = 32


def band_inverse(key, direction_sequence):
    index = jnp.arange(direction_sequence)
    distance = jnp.abs(index[:, None] - index[None, :]).astype(jnp.float32)
    length_scale = float(max(direction_sequence // 8, 2))
    ratio = math.exp(-1.0 / length_scale)
    noise = jax.random.uniform(key, (direction_sequence, direction_sequence), jnp.float32, minval=-1.0, maxval=1.0)
    return (1.0 - ratio) / (1.0 + ratio) * jnp.exp(-distance / length_scale) * (1.0 + 0.25 * noise)


def draw_inv_x(key, part):
    return band_inverse(jax.random.fold_in(key, 11), NX).astype(jnp.bfloat16)


def draw_inv_y(key, part):
    return band_inverse(jax.random.fold_in(key, 12), NY).astype(jnp.bfloat16)


def draw_inv_z(key, part):
    return band_inverse(jax.random.fold_in(key, 13), NZ).astype(jnp.bfloat16)


def draw_rate(key, part):
    lowest, highest = (0.05, 50.0)
    spread = jax.random.uniform(key, (NZ, NX, NY), jnp.float32)
    return jnp.exp(math.log(lowest) + spread * (math.log(highest) - math.log(lowest)))


def draw_hold(key, part):
    first_key, another_noise_seed, third_key = jax.random.split(key, 3)
    cruise_conditions = jax.random.uniform(first_key, (PERIOD_INTERVALS,), jnp.float32, minval=0.97, maxval=1.0)
    takeoff_surge_interval = jax.random.uniform(another_noise_seed, (PERIOD_INTERVALS,), jnp.float32, minval=0.5, maxval=0.8)
    direction_sequence = jax.random.permutation(third_key, PERIOD_INTERVALS)
    return jnp.where(direction_sequence < 2, takeoff_surge_interval, cruise_conditions)


def set_ends(result, rng, smallest, high):
    spot = [jax.random.randint(jax.random.fold_in(rng, axis), (), 0, length) for axis, length in enumerate(result.shape)]
    main_axis = result.shape.index(max(result.shape))
    next_to = spot[:main_axis] + [(spot[main_axis] + 1) % result.shape[main_axis]] + spot[main_axis + 1:]
    return result.at[tuple(spot)].set(smallest).at[tuple(next_to)].set(high)


def shard_levels(stream_key, shape, cuts, smallest, top_value):
    gain = 1.0
    for axis_at, parts in cuts:
        heights = jax.random.uniform(jax.random.fold_in(jax.random.fold_in(stream_key, 6), axis_at), (parts,), jnp.float32, smallest / len(cuts), top_value / len(cuts))
        gain = gain * jnp.repeat(jnp.exp(heights), shape[axis_at] // parts).reshape((-1,) + (1,) * (len(shape) - 1 - axis_at))
    return gain


def gaussian(key, dims, deviation, bound, cuts=(), held_as=jnp.bfloat16):
    result = jax.random.normal(key, dims, jnp.float32) * deviation
    if len(cuts) > 0:
        result = shard_levels(key, dims, cuts, -0.22, 0.18) * result
    return jnp.clip(result, min=-bound, max=bound).astype(held_as)


def setup_inputs(seed: int = 0) -> dict:
    key_of = jax.random.split(jax.random.key(seed), 12)
    return {
        "starts": gaussian(key_of[0], (PERIOD_INTERVALS, NZ, NX, NY), 1.0, 6.0, ((0, 32), (1, 16)), jnp.float32),
        "holes": set_ends((jax.random.randint(key_of[1], (NZ, NX, NY), 0, 4) < 1).astype(jnp.int32), jax.random.fold_in(key_of[1], 1), 0, 1),
        "rate": draw_rate(jax.random.fold_in(key_of[11], 71), 0),
        "zones": set_ends(jax.random.randint(key_of[3], (2, NZ, NX), 0, ZONES), jax.random.fold_in(key_of[3], 1), 0, ZONES - 1).astype(jnp.int32),
        "zone_htc": jnp.clip(jnp.exp(jax.random.uniform(key_of[4], (ZONES,), jnp.float32, math.log(0.3), math.log(4.0))), 0.3, 4.0),
        "gas": jnp.clip(-1.0 + 3.0 * jax.random.uniform(key_of[5], (PERIOD_INTERVALS, ZONES), jnp.float32) ** shard_levels(key_of[5], (PERIOD_INTERVALS, ZONES), ((0, 32),), -0.2, 0.2), -1.0, 2.0),
        "hold": draw_hold(jax.random.fold_in(key_of[11], 71), 0),
        "duration": jnp.clip(0.5 + 1.0 * jax.random.uniform(key_of[7], (PERIOD_INTERVALS,), jnp.float32) ** shard_levels(key_of[7], (PERIOD_INTERVALS,), ((0, 32),), -0.2, 0.2), 0.5, 1.5),
        "inv_x": draw_inv_x(jax.random.fold_in(key_of[11], 71), 0),
        "inv_y": draw_inv_y(jax.random.fold_in(key_of[11], 71), 0),
        "inv_z": draw_inv_z(jax.random.fold_in(key_of[11], 71), 0),
    }


COOLING = 4.0
COOLANT = -1.0
TIME_STEP = 0.2
HIGHEST = lax.Precision.HIGHEST


def conduct(values):
    return 1.0 + 0.5 * jnp.tanh(values)


def rounded(values):
    return lax.optimization_barrier(values.astype(jnp.bfloat16)).astype(jnp.float32)


def face_tables(zones, zone_htc, gas_row):
    onehot = (zones[..., None] == jnp.arange(zone_htc.shape[0], dtype=jnp.int32)).astype(zone_htc.dtype)
    return jnp.sum(onehot * zone_htc, axis=-1), jnp.sum(onehot * gas_row, axis=-1)


def step_increment(zpadded, holes, face_coef, face_temp):
    padded = jnp.pad(zpadded, ((0, 0), (1, 1), (1, 1)))
    conducts = conduct(padded)
    centre = padded[1:-1, 1:-1, 1:-1]
    centre_k = conducts[1:-1, 1:-1, 1:-1]
    neighbours = [
        (padded[2:, 1:-1, 1:-1], conducts[2:, 1:-1, 1:-1]),
        (padded[:-2, 1:-1, 1:-1], conducts[:-2, 1:-1, 1:-1]),
        (padded[1:-1, 2:, 1:-1], conducts[1:-1, 2:, 1:-1]),
        (padded[1:-1, :-2, 1:-1], conducts[1:-1, :-2, 1:-1]),
        (padded[1:-1, 1:-1, 2:], conducts[1:-1, 1:-1, 2:]),
        (padded[1:-1, 1:-1, :-2], conducts[1:-1, 1:-1, :-2]),
    ]
    flux = jnp.zeros_like(centre)
    for neighbour, neighbour_k in neighbours:
        flux = flux + 0.5 * (centre_k + neighbour_k) * (neighbour - centre)
    surface = jnp.zeros_like(centre)
    surface = surface.at[:, :, 0].add(face_coef[0] * (face_temp[0] - centre[:, :, 0]))
    surface = surface.at[:, :, -1].add(face_coef[1] * (face_temp[1] - centre[:, :, -1]))
    cooled = COOLING * holes.astype(centre.dtype) * (COOLANT - centre)
    return TIME_STEP * (flux + surface + cooled)


def across_x(inverse, values):
    return jnp.einsum('ab,zby->zay', inverse.astype(jnp.float32), rounded(values), precision=HIGHEST)


def across_y(inverse, values):
    return jnp.einsum('zxb,ab->zxa', rounded(values), inverse.astype(jnp.float32), precision=HIGHEST)


def across_z(inverse, values):
    return jnp.einsum('ab,bxy->axy', inverse.astype(jnp.float32), rounded(values), precision=HIGHEST)


def plane_steps(zpadded, holes, face_coef, face_temp, inv_x, inv_y):
    return across_y(inv_y, across_x(inv_x, step_increment(zpadded, holes, face_coef, face_temp)))


def reference(starts, holes, rate, zones, zone_htc, gas, hold, duration, inv_x, inv_y, inv_z):
    windows = starts.shape[0]

    def zpad(field):
        return jnp.pad(field, ((1, 1), (0, 0), (0, 0)))

    def fine_parts(items):
        field, gas_row, holding, length = items
        face_coef, face_temp = face_tables(zones, zone_htc, gas_row)
        planar = plane_steps(zpad(field), holes, face_coef, face_temp, inv_x, inv_y)
        vertical = across_z(inv_z, planar)
        factor = holding * jnp.exp(-rate * length / windows)
        return vertical - planar, field + vertical - factor * field

    def coarse_fix(items):
        predicted, defect, gas_row = items
        face_coef, face_temp = face_tables(zones, zone_htc, gas_row)
        planar = plane_steps(zpad(predicted), holes, face_coef, face_temp, inv_x, inv_y)
        return predicted + planar + defect

    def closing(carry, items):
        summed, length_sum, hold_prod = carry
        term, holding, length = items
        factor = holding * jnp.exp(-rate * length / windows)
        return (factor * summed + term, length_sum + length, hold_prod * holding), None

    def marching(state, items):
        term, holding, length = items
        factor = holding * jnp.exp(-rate * length / windows)
        return factor * state + term, state

    current = starts
    for sweep_index in range(ITERS):
        defects, affine_update = lax.map(fine_parts, (current, gas, hold, duration))
        zero_field = jnp.zeros_like(starts[0])
        initial = (zero_field, jnp.zeros((), starts.dtype), jnp.ones((), starts.dtype))
        (total, length_all, hold_everything), _ = lax.scan(closing, initial, (affine_update, hold, duration))
        anchor = total / (1.0 - hold_everything * jnp.exp(-rate * length_all / windows))
        _, predicted = lax.scan(marching, anchor, (affine_update, hold, duration))
        renewed = lax.map(coarse_fix, (predicted, defects, gas))
        current = jnp.roll(renewed, 1, axis=0)
    return current
```

```python
import functools

import jax
import jax.numpy as jnp
from jax import lax
from jax.experimental import pallas as pl
from jax.experimental.pallas import tpu as pltpu
from jax.sharding import PartitionSpec as P

COOLING = 4.0
COOLANT = -1.0
TIME_STEP = 0.2
MESH = pl.DeviceIdType.MESH
PIECE = 64
F32 = jnp.float32
BF16 = jnp.bfloat16


def loop(count, body):
    lax.fori_loop(0, count, lambda i, c: (body(i), c)[1], 0)


def kernel(
    T, S,
    u, holes, rate, zones, htc, gas, hold, duration, inv_x, inv_y, inv_z,
    out,
    va, vb, q, iyt, rows_tab, coef_tab, temp_tab, temp_sh, meta, meta_sh, meta_pt,
    u_sh, planar, p_sh, turned, cs, cr, es, er, aff, px, gs, gr, jm, is_, ir, ps,
    halo_s, halo_r, shift_s, shift_r, c_s, c_r, e_s, e_r, pair_s, pair_r,
    g_s, g_r, i_s, i_r, hb_s, hb_r,
):
    t, s = lax.axis_index("tm"), lax.axis_index("space")
    core = lax.rem(t, 2)
    chip = t // 2
    M = T // 2
    mate = t + 1 - 2 * core
    nt, pt = lax.rem(t + 1, T), lax.rem(t + T - 1, T)
    down, up = lax.rem(s + S - 1, S), lax.rem(s + 1, S)
    nz, nx, ny = u.shape
    xb = nx // S
    half = nz * nx // 2
    rb = half // M

    def remote(src, dst, send, recv, tt, ss):
        return pltpu.make_async_remote_copy(
            src_ref=src, dst_ref=dst, send_sem=send, recv_sem=recv,
            device_id=(tt, ss), device_id_type=MESH,
        )

    barrier = pltpu.get_barrier_semaphore()

    def greet(tt, ss):
        pl.semaphore_signal(barrier, inc=1, device_id=(tt, ss), device_id_type=MESH)

    loop(S, lambda k: greet(pt, k))
    loop(S - 1, lambda k: greet(t, lax.rem(s + 1 + k, S)))
    loop(M - 1, lambda k: greet(2 * lax.rem(chip + 1 + k, M) + core, s))
    greet(mate, s)
    greet(mate, lax.rem(s + S - 1 + 2 * core, S))

    number = htc.shape[0]
    zid = zones[...]
    coef = jnp.zeros(zid.shape, F32)
    temp = jnp.zeros(zid.shape, F32)
    for k in range(number):
        coef = jnp.where(zid == k, htc[k], coef)
        temp = jnp.where(zid == k, gas[0, k], temp)
    for tab, values in ((coef_tab, coef), (temp_tab, temp)):
        rows_tab[...] = jnp.zeros_like(rows_tab)
        for z in range(nz):
            rows_tab[2 * z : 2 * z + 1, :] = values[z : z + 1, :]
            at = (2 * z - 1) % ny
            rows_tab[at : at + 1, :] = values[nz + z : nz + z + 1, :]
        tab[...] = rows_tab[...].T
    meta[0:1, :] = jnp.full((1, ny), hold[0], F32)
    meta[1:2, :] = jnp.full((1, ny), duration[0] * (1.0 / T), F32)
    meta[2:8, :] = jnp.zeros((6, ny), F32)
    iyt[...] = inv_y[...].astype(F32).T.astype(BF16)

    pl.semaphore_wait(barrier, S + S - 1 + M - 1 + 2)

    halo = [
        remote(u.at[nz - 1], va.at[0], halo_s.at[0], halo_r.at[0], t, up),
        remote(u.at[0], va.at[nz + 1], halo_s.at[1], halo_r.at[1], t, down),
    ]
    shift = [
        remote(meta, meta_sh, shift_s.at[0], shift_r.at[0], nt, s),
        remote(temp_tab, temp_sh, shift_s.at[1], shift_r.at[1], nt, s),
        remote(u, u_sh, shift_s.at[2], shift_r.at[2], nt, s),
        remote(planar, p_sh, shift_s.at[3], shift_r.at[3], nt, s),
    ]
    for c in halo + shift[:3]:
        c.start()

    row = lax.broadcasted_iota(jnp.int32, (nx, ny), 0)
    lane = lax.broadcasted_iota(jnp.int32, (nx, ny), 1)

    def fill(v, lo, count):
        def one(i):
            z = lo + i
            q[z] = 0.5 + 0.25 * jnp.tanh(v[z])

        loop(count, one)

    def edges(v):
        v[0] = jnp.where(s > 0, v[0], 0.0)
        v[nz + 1] = jnp.where(s < S - 1, v[nz + 1], 0.0)

    def solved(v, z, temps):
        c, qc = v[z + 1], q[z + 1]
        outer = (qc + 0.5) * c
        flux = (q[z + 2] + qc) * (v[z + 2] - c) - (q[z] + qc) * (c - v[z])
        for axis, index, last in ((0, row, nx - 1), (1, lane, ny - 1)):
            n = c.shape[axis]
            vn, qn = pltpu.roll(c, n - 1, axis), pltpu.roll(qc, n - 1, axis)
            ahead = jnp.where(index == last, -outer, (qn + qc) * (vn - c))
            behind = jnp.where(index == 0, outer, pltpu.roll(ahead, 1, axis))
            flux = flux + ahead - behind
        turn = lax.rem(ny - 2 * z, ny)
        face_coef = pltpu.roll(coef_tab[...], turn, 1)
        face_temp = pltpu.roll(temps[...], turn, 1)
        on_face = (lane == 0) | (lane == ny - 1)
        surface = jnp.where(on_face, face_coef * (face_temp - c), 0.0)
        cooled = COOLING * holes[z].astype(F32) * (COOLANT - c)
        e = (TIME_STEP * (flux + surface + cooled)).astype(BF16)
        x = jnp.dot(inv_x[...], e, preferred_element_type=F32).astype(BF16)
        return c, jnp.dot(x, iyt[...], preferred_element_type=F32)

    def own_copy(i):
        va[i + 1] = u[i]

    loop(nz, own_copy)
    fill(va, 1, nz)
    halo[0].wait_recv()
    halo[1].wait_recv()
    edges(va)
    q[0] = 0.5 + 0.25 * jnp.tanh(va[0])
    q[nz + 1] = 0.5 + 0.25 * jnp.tanh(va[nz + 1])

    def first(z):
        _, p = solved(va, z, temp_tab)
        planar[z] = p
        turned[pl.ds(z, nx, stride=nz), :] = p

    loop(nz, first)

    def c_copy(k):
        to = lax.rem(s + 1 + k, S)
        return remote(
            cs.at[pl.ds(to * xb, xb)], cr.at[s], c_s.at[to], c_r.at[s], nt, to
        )

    def c_send(k):
        to = lax.rem(s + 1 + k, S)
        block = turned[pl.ds(to * (xb * nz), xb * nz), :]
        cs[pl.ds(to * xb, xb)] = block.reshape(xb, nz, ny).astype(BF16)
        c_copy(k).start()

    loop(S, c_send)
    shift[3].start()

    shift[0].wait_recv()
    mates = remote(meta_sh, meta_pt, pair_s.at[0], pair_r.at[0], mate, s)
    mates.start()
    shift[2].wait_recv()

    def decay(m, rows):
        return m[0:1, :] * jnp.exp(-(rate[rows, :] * m[1:2, :]))

    def base(i):
        rows = pl.ds(pl.multiple_of(i * nx, nx), nx)
        field = u_sh[i]
        aff[rows, :] = field - decay(meta_sh, rows) * field

    loop(nz, base)

    def c_wait(k):
        remote(cs.at[pl.ds(0, xb)], cr.at[k], c_s.at[k], c_r.at[k], nt, k).wait_recv()

    loop(S, c_wait)
    for x in range(xb):
        lines = cr[:, x].reshape(S * nz, ny)
        es[pl.ds(x, S * nz, stride=xb), :] = jnp.dot(
            inv_z[...], lines, preferred_element_type=F32
        )

    blk = nz * xb

    def e_copy(k):
        to = lax.rem(s + 1 + k, S)
        return remote(es.at[pl.ds(to * blk, blk)], er.at[s], e_s.at[to], e_r.at[s], t, to)

    loop(S - 1, lambda k: e_copy(k).start())
    er[s] = es[pl.ds(s * blk, blk), :]

    def e_wait(k):
        frm = lax.rem(s + 1 + k, S)
        remote(es.at[pl.ds(0, blk)], er.at[frm], e_s.at[frm], e_r.at[frm], t, frm).wait_recv()

    loop(S - 1, e_wait)

    def vertical(z):
        return er[:, pl.ds(pl.multiple_of(z * xb, xb), xb), :].reshape(nx, ny)

    def affine(z):
        rows = pl.ds(pl.multiple_of(z * nx, nx), nx)
        aff[rows, :] = aff[rows, :] + vertical(z)

    loop(nz, affine)
    swap = remote(
        aff.at[pl.ds((1 - core) * half, half)], px, pair_s.at[1], pair_r.at[1], mate, s
    )
    swap.start()
    mates.wait_recv()
    low = jnp.where(core == 0, meta_sh[...], meta_pt[...])
    high = jnp.where(core == 0, meta_pt[...], meta_sh[...])
    both = jnp.concatenate(
        [low[0:1] * high[0:1], low[1:2] + high[1:2], jnp.zeros((6, ny), F32)], axis=0
    )
    swap.wait_recv()

    def place(i):
        return i // (rb // PIECE), lax.rem(i, rb // PIECE) * PIECE

    def pieces(i):
        mine = pl.ds(pl.multiple_of(core * half + i * PIECE, PIECE), PIECE)
        theirs = pl.ds(pl.multiple_of(i * PIECE, PIECE), PIECE)
        own, other = aff[mine, :], px[theirs, :]
        return mine, jnp.where(core == 0, own, other), jnp.where(core == 0, other, own)

    def composed(i):
        block, at = place(i)
        mine, lo, hi = pieces(i)
        gs[block, pl.ds(pl.multiple_of(at, PIECE), PIECE), :] = decay(high, mine) * lo + hi

    loop(half // PIECE, composed)

    def add_meta(k):
        gs[k, rb : rb + 8, :] = both

    loop(M, add_meta)

    def g_copy(k):
        to = lax.rem(chip + 1 + k, M)
        return remote(gs.at[to], gr.at[chip], g_s.at[to], g_r.at[chip], 2 * to + core, s)

    loop(M - 1, lambda k: g_copy(k).start())
    gr[chip] = gs[chip]

    def g_wait(k):
        frm = lax.rem(chip + 1 + k, M)
        remote(gs.at[0], gr.at[frm], g_s.at[frm], g_r.at[frm], 2 * frm + core, s).wait_recv()

    loop(M - 1, g_wait)

    def scan(i):
        at = pl.ds(pl.multiple_of(i * PIECE, PIECE), PIECE)
        speed = rate[pl.ds(pl.multiple_of(core * half + chip * rb + i * PIECE, PIECE), PIECE), :]

        def close(m, carry):
            total, kept, length = carry
            h, d = gr[m, rb : rb + 1, :], gr[m, rb + 1 : rb + 2, :]
            factor = h * jnp.exp(-(speed * d))
            jm[m, at, :] = factor
            return factor * total + gr[m, at, :], kept * h, length + d

        total, kept, length = lax.fori_loop(
            0, M, close,
            (jnp.zeros((PIECE, ny), F32), jnp.ones((1, ny), F32), jnp.zeros((1, ny), F32)),
        )

        def march(m, state):
            is_[m, at, :] = state
            return jm[m, at, :] * state + gr[m, at, :]

        lax.fori_loop(0, M, march, total / (1.0 - kept * jnp.exp(-(speed * length))))

    loop(rb // PIECE, scan)

    def i_copy(k):
        to = lax.rem(chip + 1 + k, M)
        return remote(is_.at[to], ir.at[chip], i_s.at[to], i_r.at[chip], 2 * to + core, s)

    loop(M - 1, lambda k: i_copy(k).start())
    ir[chip] = is_[chip]

    def i_wait(k):
        frm = lax.rem(chip + 1 + k, M)
        remote(is_.at[0], ir.at[frm], i_s.at[frm], i_r.at[frm], 2 * frm + core, s).wait_recv()

    loop(M - 1, i_wait)


    def predict(i):
        block, at = place(i)
        mine, lo, _ = pieces(i)
        p0 = ir[block, pl.ds(pl.multiple_of(at, PIECE), PIECE), :]
        p1 = decay(low, mine) * p0 + lo
        z = core * (nz // 2) + i // (nx // PIECE)
        within = pl.ds(pl.multiple_of(lax.rem(i, nx // PIECE) * PIECE, PIECE), PIECE)
        vb[z + 1, within, :] = jnp.where(core == 0, p0, p1)
        ps[i // (nx // PIECE), within, :] = jnp.where(core == 0, p1, p0)

    loop(half // PIECE, predict)
    beside = lax.rem(s + S - 1 + 2 * core, S)
    edge = (1 - core) * (nz + 1)
    hb = [
        remote(
            vb.at[1 + core * (nz - 1)], vb.at[edge], hb_s.at[0], hb_r.at[1 - core], t, beside
        ),
        remote(
            ps.at[core * (nz // 2 - 1)], vb.at[edge], hb_s.at[1], hb_r.at[1 - core], mate, beside
        ),
    ]
    give = remote(
        ps, vb.at[pl.ds(1 + core * (nz // 2), nz // 2)], pair_s.at[2], pair_r.at[2], mate, s
    )
    for c in hb + [give]:
        c.start()
    fill(vb, 1 + core * (nz // 2), nz // 2)
    give.wait_recv()
    fill(vb, 1 + (1 - core) * (nz // 2), nz // 2)
    for side in range(2):
        remote(
            ps.at[0], vb.at[side * (nz + 1)], hb_s.at[side], hb_r.at[side], t, beside
        ).wait_recv()
    edges(vb)
    q[0] = 0.5 + 0.25 * jnp.tanh(vb[0])
    q[nz + 1] = 0.5 + 0.25 * jnp.tanh(vb[nz + 1])
    shift[1].wait_recv()
    shift[3].wait_recv()

    def second(z):
        c, p = solved(vb, z, temp_sh)
        out[z] = c + p + (vertical(z) - p_sh[z])

    loop(nz, second)

    for c in halo + shift + [mates, swap, give] + hb:
        c.wait_send()
    loop(S, lambda k: c_copy(k).wait_send())
    loop(S - 1, lambda k: e_copy(k).wait_send())
    loop(M - 1, lambda k: g_copy(k).wait_send())
    loop(M - 1, lambda k: i_copy(k).wait_send())


def per_device(T, S, starts, holes, rate, zones, htc, gas, hold, duration, inv_x, inv_y, inv_z):
    _, nz, nx, ny = starts.shape
    xb, M = nx // S, T // 2
    half = nz * nx // 2
    rb = half // M
    vmem = pl.BlockSpec(memory_space=pltpu.VMEM)
    smem = pl.BlockSpec(memory_space=pltpu.SMEM)
    dma = lambda n: pltpu.SemaphoreType.DMA((n,))
    v32 = lambda *shape: pltpu.VMEM(shape, F32)
    result = pl.pallas_call(
        functools.partial(kernel, T, S),
        out_shape=jax.ShapeDtypeStruct((nz, nx, ny), F32),
        in_specs=[vmem, vmem, vmem, vmem, smem, smem, smem, smem, vmem, vmem, vmem],
        out_specs=vmem,
        scratch_shapes=[
            v32(nz + 2, nx, ny), v32(nz + 2, nx, ny), v32(nz + 2, nx, ny),
            pltpu.VMEM((ny, ny), BF16),
            v32(ny, nx), v32(nx, ny), v32(nx, ny), v32(nx, ny),
            v32(8, ny), v32(8, ny), v32(8, ny),
            v32(nz, nx, ny), v32(nz, nx, ny), v32(nz, nx, ny),
            v32(nx * nz, ny),
            pltpu.VMEM((nx, nz, ny), BF16),
            pltpu.VMEM((S, xb, nz, ny), BF16),
            v32(S * nz * xb, ny), v32(S, nz * xb, ny),
            v32(nz * nx, ny), v32(half, ny),
            v32(M, rb + 8, ny), v32(M, rb + 8, ny), v32(M, rb, ny),
            v32(M, rb, ny), v32(M, rb, ny), v32(nz // 2, nx, ny),
            dma(2), dma(2), dma(4), dma(4), dma(S), dma(S), dma(S), dma(S), dma(3), dma(3),
            dma(M), dma(M), dma(M), dma(M), dma(2), dma(2),
        ],
        compiler_params=pltpu.CompilerParams(
            collective_id=0, has_side_effects=True, vmem_limit_bytes=48 * 1024 * 1024
        ),
    )(
        starts[0], holes, rate.reshape(nz * nx, ny), zones.reshape(2 * nz, nx),
        htc, gas, hold, duration, inv_x, inv_y, inv_z,
    )
    return result[None]


def solution(mesh):
    return jax.shard_map(
        functools.partial(per_device, mesh.shape["tm"], mesh.shape["space"]),
        mesh=mesh,
        in_specs=(
            P("tm", "space", None, None),
            P("space", None, None),
            P("space", None, None),
            P(None, "space", None),
            P(),
            P("tm", None),
            P("tm"),
            P("tm"),
            P(),
            P(),
            P(),
        ),
        out_specs=P("tm", "space", None, None),
        check_vma=False,
    )
```

```python
import functools

import jax
import jax.numpy as jnp
from jax import lax
from jax.experimental import pallas as pl
from jax.experimental.pallas import tpu as pltpu
from jax.sharding import PartitionSpec as P

COOLING = 4.0
COOLANT = -1.0
TIME_STEP = 0.2
MESH = pl.DeviceIdType.MESH
PIECE = 64
F32 = jnp.float32
BF16 = jnp.bfloat16


def loop(count, body):
    lax.fori_loop(0, count, lambda i, c: (body(i), c)[1], 0)


def kernel(
    T, S,
    u_in, holes_in, rate_in, zones_in, htc, gas, hold, duration, inv_x_in, inv_y_in, inv_z_in,
    out,
    u, holes, rate, zones, inv_x, inv_y, inv_z, load_s,
    va, vb, q, iyt, rows_tab, coef_tab, temp_tab, temp_sh, meta, meta_sh, meta_pt,
    u_sh, planar, turned, cs, cr, es, aff, px, ver, ps, jm, gf,
    p_q, p_u, psh_q, psh_u, eq, eu, er_q, er_u, gs_q, gs_u, gr_q, gr_u, is_q, is_u, ir_q, ir_u,
    halo_s, halo_r, shift_s, shift_r, c_s, c_r, e_s, e_r, pair_s, pair_r,
    g_s, g_r, i_s, i_r, hb_s, hb_r,
):
    t, s = lax.axis_index("tm"), lax.axis_index("space")
    core = lax.rem(t, 2)
    chip = t // 2
    M = T // 2
    mate = t + 1 - 2 * core
    nt, pt = lax.rem(t + 1, T), lax.rem(t + T - 1, T)
    down, up = lax.rem(s + S - 1, S), lax.rem(s + 1, S)
    nz, nx, ny = u.shape
    xb = nx // S
    half = nz * nx // 2
    rb = half // M

    def remote(src, dst, send, recv, tt, ss):
        return pltpu.make_async_remote_copy(
            src_ref=src, dst_ref=dst, send_sem=send, recv_sem=recv,
            device_id=(tt, ss), device_id_type=MESH,
        )

    loads = [
        pltpu.make_async_copy(src, dst, load_s.at[i])
        for i, (src, dst) in enumerate(
            (
                (zones_in, zones), (u_in, u), (inv_y_in, inv_y), (inv_x_in, inv_x),
                (holes_in, holes), (rate_in, rate), (inv_z_in, inv_z),
            )
        )
    ]
    for c in loads:
        c.start()

    barrier = pltpu.get_barrier_semaphore()

    def greet(tt, ss):
        pl.semaphore_signal(barrier, inc=1, device_id=(tt, ss), device_id_type=MESH)

    loop(S, lambda k: greet(pt, k))
    loop(S - 1, lambda k: greet(t, lax.rem(s + 1 + k, S)))
    loop(M - 1, lambda k: greet(2 * lax.rem(chip + 1 + k, M) + core, s))
    greet(mate, s)
    greet(mate, lax.rem(s + S - 1 + 2 * core, S))

    number = htc.shape[0]
    loads[0].wait()
    zid = zones[...]
    coef = jnp.zeros(zid.shape, F32)
    temp = jnp.zeros(zid.shape, F32)
    for k in range(number):
        coef = jnp.where(zid == k, htc[k], coef)
        temp = jnp.where(zid == k, gas[0, k], temp)
    for tab, values in ((coef_tab, coef), (temp_tab, temp)):
        rows_tab[...] = jnp.zeros_like(rows_tab)
        for z in range(nz):
            rows_tab[2 * z : 2 * z + 1, :] = values[z : z + 1, :]
            at = (2 * z - 1) % ny
            rows_tab[at : at + 1, :] = values[nz + z : nz + z + 1, :]
        tab[...] = rows_tab[...].T
    meta[0:1, :] = jnp.full((1, ny), hold[0], F32)
    meta[1:2, :] = jnp.full((1, ny), duration[0] * (1.0 / T), F32)
    meta[2:8, :] = jnp.zeros((6, ny), F32)
    for c in loads[1:]:
        c.wait()
    iyt[...] = inv_y[...].astype(F32).T.astype(BF16)

    pl.semaphore_wait(barrier, S + S - 1 + M - 1 + 2)

    halo = [
        remote(u.at[nz - 1], va.at[0], halo_s.at[0], halo_r.at[0], t, up),
        remote(u.at[0], va.at[nz + 1], halo_s.at[1], halo_r.at[1], t, down),
    ]
    shift = [
        remote(meta, meta_sh, shift_s.at[0], shift_r.at[0], nt, s),
        remote(temp_tab, temp_sh, shift_s.at[1], shift_r.at[1], nt, s),
        remote(u, u_sh, shift_s.at[2], shift_r.at[2], nt, s),
        remote(p_q, psh_q, shift_s.at[3], shift_r.at[3], nt, s),
        remote(p_u, psh_u, shift_s.at[4], shift_r.at[4], nt, s),
    ]
    for c in halo + shift[:3]:
        c.start()

    row = lax.broadcasted_iota(jnp.int32, (nx, ny), 0)
    lane = lax.broadcasted_iota(jnp.int32, (nx, ny), 1)

    def conductivity(v):
        return 0.5 + 0.25 * jnp.tanh(v)

    def fill(v, lo, count):
        def one(i):
            q[lo + i] = conductivity(v[lo + i])

        loop(count, one)

    def edges(v):
        v[0] = jnp.where(s > 0, v[0], 0.0)
        v[nz + 1] = jnp.where(s < S - 1, v[nz + 1], 0.0)
        q[0] = conductivity(v[0])
        q[nz + 1] = conductivity(v[nz + 1])

    def solved(v, z, temps):
        c, qc = v[z + 1], q[z + 1]
        outer = (qc + 0.5) * c
        flux = (q[z + 2] + qc) * (v[z + 2] - c) - (q[z] + qc) * (c - v[z])
        for axis, index, last in ((0, row, nx - 1), (1, lane, ny - 1)):
            n = c.shape[axis]
            vn, qn = pltpu.roll(c, n - 1, axis), pltpu.roll(qc, n - 1, axis)
            ahead = jnp.where(index == last, -outer, (qn + qc) * (vn - c))
            behind = jnp.where(index == 0, outer, pltpu.roll(ahead, 1, axis))
            flux = flux + ahead - behind
        turn = lax.rem(ny - 2 * z, ny)
        face_coef = pltpu.roll(coef_tab[...], turn, 1)
        face_temp = pltpu.roll(temps[...], turn, 1)
        on_face = (lane == 0) | (lane == ny - 1)
        surface = jnp.where(on_face, face_coef * (face_temp - c), 0.0)
        cooled = COOLING * holes[z].astype(F32) * (COOLANT - c)
        e = (TIME_STEP * (flux + surface + cooled)).astype(BF16)
        x = jnp.dot(inv_x[...], e, preferred_element_type=F32).astype(BF16)
        return c, jnp.dot(x, iyt[...], preferred_element_type=F32)

    def coded(v):
        top = jnp.max(jnp.abs(v), axis=0, keepdims=True)
        unit = jnp.maximum(top, 1e-30) * (1.0 / 32767.0)
        steps = jnp.round(v * (1.0 / unit))
        return steps.astype(jnp.int32).astype(jnp.int16), unit

    def decoded(steps, unit):
        return steps.astype(jnp.int32).astype(F32) * unit

    def own_copy(i):
        field = u[i]
        va[i + 1] = field
        q[i + 1] = conductivity(field)

    loop(nz, own_copy)

    def keep(z, p):
        planar[z] = p
        turned[pl.ds(z, nx, stride=nz), :] = p

    def first(i):
        z = 1 + 2 * i
        _, p = solved(va, z, temp_tab)
        _, r = solved(va, z + 1, temp_tab)
        keep(z, p)
        keep(z + 1, r)

    loop((nz - 2) // 2, first)
    halo[0].wait_recv()
    halo[1].wait_recv()
    edges(va)
    for z in (0, nz - 1):
        keep(z, solved(va, z, temp_tab)[1])

    def c_copy(k):
        to = lax.rem(s + 1 + k, S)
        return remote(
            cs.at[pl.ds(to * xb, xb)], cr.at[s], c_s.at[to], c_r.at[s], t, to
        )

    def c_block(to):
        block = turned[pl.ds(to * (xb * nz), xb * nz), :]
        return block.reshape(xb, nz, ny).astype(BF16)

    def c_send(k):
        to = lax.rem(s + 1 + k, S)
        cs[pl.ds(to * xb, xb)] = c_block(to)
        c_copy(k).start()

    loop(S - 1, c_send)
    cr[s] = c_block(s)

    def p_code(z):
        p_q[z], p_u[z] = coded(planar[z])

    loop(nz, p_code)
    shift[3].start()
    shift[4].start()
    shift[0].wait_recv()
    mates = remote(meta_sh, meta_pt, pair_s.at[0], pair_r.at[0], mate, s)
    mates.start()
    shift[2].wait_recv()
    per = PIECE // xb

    def decay(m, rows):
        return m[0:1, :] * jnp.exp(-(rate[rows, :] * m[1:2, :]))

    def base(i):
        field = u_sh[i]
        rows = pl.ds(pl.multiple_of(i * nx, nx), nx)
        aff[i] = (field - decay(meta_sh, rows) * field).reshape(S, xb, ny)

    loop(nz, base)

    def c_wait(k):
        frm = lax.rem(s + 1 + k, S)
        remote(cs.at[pl.ds(0, xb)], cr.at[frm], c_s.at[frm], c_r.at[frm], t, frm).wait_recv()

    loop(S - 1, c_wait)
    for x in range(xb):
        lines = cr[:, x].reshape(S * nz, ny)
        es[pl.ds(x, S * nz, stride=xb), :] = jnp.dot(
            inv_z[...], lines, preferred_element_type=F32
        )

    blk = nz * xb

    def e_copies(k):
        to = lax.rem(s + 1 + k, S)
        return (
            remote(eq.at[to], er_q.at[s], e_s.at[to], e_r.at[s], nt, to),
            remote(eu.at[to], er_u.at[s], e_s.at[S + to], e_r.at[S + s], nt, to),
        )

    def e_send(k):
        to = lax.rem(s + 1 + k, S)
        eq[to], eu[to] = coded(es[pl.ds(pl.multiple_of(to * blk, blk), blk), :])
        for c in e_copies(k):
            c.start()

    loop(S, e_send)

    def e_take(k):
        frm = lax.rem(s + 1 + k, S)
        remote(eq.at[0], er_q.at[frm], e_s.at[frm], e_r.at[frm], nt, frm).wait_recv()
        remote(eu.at[0], er_u.at[frm], e_s.at[frm], e_r.at[S + frm], nt, frm).wait_recv()
        part = decoded(er_q[frm], er_u[frm]).reshape(nz, xb, ny)
        ver[:, frm] = part
        aff[:, frm] = aff[:, frm] + part

    loop(S, e_take)
    swap = remote(
        aff.at[pl.ds((1 - core) * (nz // 2), nz // 2)], px, pair_s.at[1], pair_r.at[1], mate, s
    )
    swap.start()
    mates.wait_recv()
    low = jnp.where(core == 0, meta_sh[...], meta_pt[...])
    high = jnp.where(core == 0, meta_pt[...], meta_sh[...])
    swap.wait_recv()

    def pieces(i):
        mine = pl.ds(pl.multiple_of(core * half + i * PIECE, PIECE), PIECE)
        z, at = i // (nx // PIECE), lax.rem(i, nx // PIECE) * per
        own = aff[core * (nz // 2) + z, pl.ds(at, per)].reshape(PIECE, ny)
        other = px[z, pl.ds(at, per)].reshape(PIECE, ny)
        return mine, jnp.where(core == 0, own, other), jnp.where(core == 0, other, own)

    each = rb // PIECE

    def g_copies(k):
        to = lax.rem(chip + 1 + k, M)
        there = 2 * to + core
        return (
            remote(gs_q.at[to], gr_q.at[chip], g_s.at[to], g_r.at[chip], there, s),
            remote(gs_u.at[to], gr_u.at[chip], g_s.at[M + to], g_r.at[M + chip], there, s),
        )

    def g_block(to):
        for j in range(each):
            mine, lo, hi = pieces(to * each + j)
            steps, unit = coded(decay(high, mine) * lo + hi)
            gs_q[to, j] = steps
            gs_u[to, j] = jnp.concatenate(
                [low[0:1] * high[0:1], low[1:2] + high[1:2], unit, unit], axis=0
            )

    def g_send(k):
        g_block(lax.rem(chip + 1 + k, M))
        for c in g_copies(k):
            c.start()

    loop(M - 1, g_send)
    g_block(chip)
    gr_q[chip] = gs_q[chip]
    gr_u[chip] = gs_u[chip]

    def speed(j):
        return rate[pl.ds(pl.multiple_of(core * half + chip * rb + j * PIECE, PIECE), PIECE), :]

    def g_wait(k):
        frm = lax.rem(chip + 1 + k, M)
        there = 2 * frm + core
        remote(gs_q.at[0], gr_q.at[frm], g_s.at[frm], g_r.at[frm], there, s).wait_recv()
        remote(gs_u.at[0], gr_u.at[frm], g_s.at[frm], g_r.at[M + frm], there, s).wait_recv()

    shift[1].wait_recv()
    shift[3].wait_recv()
    shift[4].wait_recv()

    def defect(z):
        ver[z] = ver[z] - decoded(psh_q[z], psh_u[z]).reshape(S, xb, ny)

    loop(nz, defect)
    loop(M - 1, g_wait)

    def i_copies(to):
        there = 2 * to + core
        return (
            remote(is_q.at[to], ir_q.at[chip], i_s.at[to], i_r.at[chip], there, s),
            remote(is_u.at[to], ir_u.at[chip], i_s.at[M + to], i_r.at[M + chip], there, s),
        )

    totals = []
    for j in range(each):

        def close(m, carry, j=j):
            total, kept, length = carry
            h, d = gr_u[m, j, 0:1], gr_u[m, j, 1:2]
            factor = h * jnp.exp(-(speed(j) * d))
            term = decoded(gr_q[m, j], gr_u[m, j, 2:3])
            jm[m, j] = factor
            gf[m, j] = term
            return factor * total + term, kept * h, length + d

        total, kept, length = lax.fori_loop(
            0, M, close,
            (jnp.zeros((PIECE, ny), F32), jnp.ones((1, ny), F32), jnp.zeros((1, ny), F32)),
        )
        totals.append(total / (1.0 - kept * jnp.exp(-(speed(j) * length))))

    def march(m, states):
        for j in range(each):
            is_q[m, j], is_u[m, j] = coded(states[j])

        @pl.when(m != chip)
        def _():
            for c in i_copies(m):
                c.start()

        return tuple(jm[m, j] * states[j] + gf[m, j] for j in range(each))

    lax.fori_loop(0, M, march, tuple(totals))
    ir_q[chip] = is_q[chip]
    ir_u[chip] = is_u[chip]

    def predict(i):
        block, j = i // each, lax.rem(i, each)
        mine, lo, _ = pieces(i)
        p0 = decoded(ir_q[block, j], ir_u[block, j])
        p1 = decay(low, mine) * p0 + lo
        z = i // (nx // PIECE)
        within = pl.ds(pl.multiple_of(lax.rem(i, nx // PIECE) * PIECE, PIECE), PIECE)
        kept = jnp.where(core == 0, p0, p1)
        vb[core * (nz // 2) + z + 1, within, :] = kept
        q[core * (nz // 2) + z + 1, within, :] = conductivity(kept)
        ps[z, within, :] = jnp.where(core == 0, p1, p0)

    def i_take(k):
        frm = lax.rem(chip + 1 + k, M)
        there = 2 * frm + core
        remote(is_q.at[0], ir_q.at[frm], i_s.at[frm], i_r.at[frm], there, s).wait_recv()
        remote(is_u.at[0], ir_u.at[frm], i_s.at[frm], i_r.at[M + frm], there, s).wait_recv()
        for j in range(each):
            predict(frm * each + j)

    loop(M - 1, i_take)
    for j in range(each):
        predict(chip * each + j)
    beside = lax.rem(s + S - 1 + 2 * core, S)
    edge = (1 - core) * (nz + 1)
    hb = [
        remote(
            ps.at[core * (nz // 2 - 1)], vb.at[edge], hb_s.at[1], hb_r.at[1 - core], mate, beside
        ),
        remote(
            vb.at[1 + core * (nz - 1)], vb.at[edge], hb_s.at[0], hb_r.at[1 - core], t, beside
        ),
    ]
    give = remote(
        ps, vb.at[pl.ds(1 + core * (nz // 2), nz // 2)], pair_s.at[2], pair_r.at[2], mate, s
    )
    for c in hb + [give]:
        c.start()

    def second(i):
        z0 = lax.rem(core * (nz // 2) + 1 + 2 * i, nz)
        z1 = lax.rem(core * (nz // 2) + 2 + 2 * i, nz)
        c0, p = solved(vb, z0, temp_sh)
        c1, r = solved(vb, z1, temp_sh)
        out[z0] = c0 + p + ver[z0].reshape(nx, ny)
        out[z1] = c1 + r + ver[z1].reshape(nx, ny)

    inner = nz // 4 - 1
    loop(inner, second)
    give.wait_recv()
    fill(vb, 1 + (1 - core) * (nz // 2), nz // 2)
    for side in range(2):
        remote(
            ps.at[0], vb.at[side * (nz + 1)], hb_s.at[side], hb_r.at[side], t, beside
        ).wait_recv()
    edges(vb)
    loop(nz // 2 - inner, lambda i: second(i + inner))

    for c in halo + shift + [mates, swap, give] + hb:
        c.wait_send()
    loop(S - 1, lambda k: c_copy(k).wait_send())

    def sent(copies):
        for c in copies:
            c.wait_send()

    loop(S, lambda k: sent(e_copies(k)))
    loop(M - 1, lambda k: sent(g_copies(k)))
    loop(M - 1, lambda k: sent(i_copies(lax.rem(chip + 1 + k, M))))


def per_device(T, S, starts, holes, rate, zones, htc, gas, hold, duration, inv_x, inv_y, inv_z):
    _, nz, nx, ny = starts.shape
    xb, M = nx // S, T // 2
    half = nz * nx // 2
    each = half // M // PIECE
    vmem = pl.BlockSpec(memory_space=pltpu.VMEM)
    hbm = pl.BlockSpec(memory_space=pltpu.HBM)
    smem = pl.BlockSpec(memory_space=pltpu.SMEM)
    dma = lambda n: pltpu.SemaphoreType.DMA((n,))
    i16 = lambda *shape: pltpu.VMEM(shape, jnp.int16)
    v32 = lambda *shape: pltpu.VMEM(shape, F32)
    result = pl.pallas_call(
        functools.partial(kernel, T, S),
        out_shape=jax.ShapeDtypeStruct((nz, nx, ny), F32),
        in_specs=[hbm, hbm, hbm, hbm, smem, smem, smem, smem, hbm, hbm, hbm],
        out_specs=vmem,
        scratch_shapes=[
            v32(nz, nx, ny), pltpu.VMEM((nz, nx, ny), jnp.int32), v32(nz * nx, ny),
            pltpu.VMEM((2 * nz, nx), jnp.int32), pltpu.VMEM((nx, nx), BF16),
            pltpu.VMEM((ny, ny), BF16), pltpu.VMEM((S * nz, S * nz), BF16), dma(7),
            v32(nz + 2, nx, ny), v32(nz + 2, nx, ny), v32(nz + 2, nx, ny),
            pltpu.VMEM((ny, ny), BF16),
            v32(ny, nx), v32(nx, ny), v32(nx, ny), v32(nx, ny),
            v32(8, ny), v32(8, ny), v32(8, ny),
            v32(nz, nx, ny), v32(nz, nx, ny), v32(nx * nz, ny),
            pltpu.VMEM((nx, nz, ny), BF16), pltpu.VMEM((S, xb, nz, ny), BF16),
            v32(S * nz * xb, ny), v32(nz, S, xb, ny), v32(nz // 2, S, xb, ny),
            v32(nz, S, xb, ny), v32(nz // 2, nx, ny),
            v32(M, each, PIECE, ny), v32(M, each, PIECE, ny),
            i16(nz, nx, ny), v32(nz, 1, ny), i16(nz, nx, ny), v32(nz, 1, ny),
            i16(S, nz * xb, ny), v32(S, 1, ny), i16(S, nz * xb, ny), v32(S, 1, ny),
            i16(M, each, PIECE, ny), v32(M, each, 4, ny), i16(M, each, PIECE, ny), v32(M, each, 4, ny),
            i16(M, each, PIECE, ny), v32(M, each, 1, ny), i16(M, each, PIECE, ny), v32(M, each, 1, ny),
            dma(2), dma(2), dma(5), dma(5), dma(S), dma(S), dma(2 * S), dma(2 * S), dma(3), dma(3),
            dma(2 * M), dma(2 * M), dma(2 * M), dma(2 * M), dma(2), dma(2),
        ],
        compiler_params=pltpu.CompilerParams(
            collective_id=0, has_side_effects=True, vmem_limit_bytes=60 * 1024 * 1024
        ),
    )(
        starts[0], holes, rate.reshape(nz * nx, ny), zones.reshape(2 * nz, nx),
        htc, gas, hold, duration, inv_x, inv_y, inv_z,
    )
    return result[None]


def solution(mesh):
    return jax.shard_map(
        functools.partial(per_device, mesh.shape["tm"], mesh.shape["space"]),
        mesh=mesh,
        in_specs=(
            P("tm", "space", None, None),
            P("space", None, None),
            P("space", None, None),
            P(None, "space", None),
            P(),
            P("tm", None),
            P("tm"),
            P("tm"),
            P(),
            P(),
            P(),
        ),
        out_specs=P("tm", "space", None, None),
        check_vma=False,
    )
```

```python
import functools

import jax
import jax.numpy as jnp
from jax import lax
from jax.experimental import pallas as pl
from jax.experimental.pallas import tpu as pltpu
from jax.sharding import PartitionSpec as P

COOLING = 4.0
COOLANT = -1.0
TIME_STEP = 0.2
MESH = pl.DeviceIdType.MESH
F32 = jnp.float32
BF16 = jnp.bfloat16


def loop(count, body):
    lax.fori_loop(0, count, lambda i, c: (body(i), c)[1], 0)


def kernel(
    T, S,
    u_in, holes_in, rate_in, zones_in, htc, gas, hold, duration, inv_x_in, inv_y_in, inv_z_in,
    out_q, out_u,
    u, holes, rate, zones, inv_x, inv_y, inv_z, load_s,
    va, vb, q, iyt, rows_tab, coef_tab, temp_tab, meta, meta_pt,
    planar, turned, cs, cr, es, aff, px, ver, ps, jm, gf,
    eq, eu, er_q, er_u, gs_q, gs_u, gr_q, gr_u, is_q, is_u, ir_q, ir_u, oq, ou,
    halo_s, halo_r, meta_s, meta_r, c_s, c_r, e_s, e_r, swap_s, swap_r,
    g_s, g_r, i_s, i_r, give_s, give_r, hb_s, hb_r, o_s, o_r,
):
    t, s = lax.axis_index("tm"), lax.axis_index("space")
    core = lax.rem(t, 2)
    chip = t // 2
    M, H = T // 2, S // 2
    mate = t + 1 - 2 * core
    nt, pt = lax.rem(t + 1, T), lax.rem(t + T - 1, T)
    down, up = lax.rem(s + S - 1, S), lax.rem(s + 1, S)
    nz, nx, ny = u.shape
    xb = nx // S
    blk = nz * xb
    rb = nz * nx // 2 // M
    zr = rb // xb
    ratio = blk // rb
    base_x = core * (nx // 2)

    def remote(src, dst, send, recv, tt, ss):
        return pltpu.make_async_remote_copy(
            src_ref=src, dst_ref=dst, send_sem=send, recv_sem=recv,
            device_id=(tt, ss), device_id_type=MESH,
        )

    loads = [
        pltpu.make_async_copy(src, dst, load_s.at[i])
        for i, (src, dst) in enumerate(
            (
                (u_in, u), (zones_in, zones), (inv_y_in, inv_y), (inv_x_in, inv_x),
                (holes_in, holes), (rate_in, rate), (inv_z_in, inv_z),
            )
        )
    ]
    for c in loads:
        c.start()

    barrier = pltpu.get_barrier_semaphore()

    def greet(tt, ss):
        pl.semaphore_signal(barrier, inc=1, device_id=(tt, ss), device_id_type=MESH)

    loop(S - 1, lambda k: greet(t, lax.rem(s + 1 + k, S)))
    loop(M - 1, lambda k: greet(2 * lax.rem(chip + 1 + k, M) + core, s))
    greet(mate, s)
    greet(mate, down)
    greet(mate, up)
    greet(pt, s)
    loads[0].wait()
    pl.semaphore_wait(barrier, S - 1 + M - 1 + 4)

    halo = [
        remote(u.at[nz - 1], va.at[0], halo_s.at[0], halo_r.at[0], t, up),
        remote(u.at[0], va.at[nz + 1], halo_s.at[1], halo_r.at[1], t, down),
    ]
    for c in halo:
        c.start()
    meta[0:1, :] = jnp.full((1, ny), hold[0], F32)
    meta[1:2, :] = jnp.full((1, ny), duration[0] * (1.0 / T), F32)
    meta[2:8, :] = jnp.zeros((6, ny), F32)
    mates = remote(meta, meta_pt, meta_s.at[0], meta_r.at[0], mate, s)
    mates.start()

    for c in loads[1:]:
        c.wait()
    zid = zones[...]
    coef = jnp.zeros(zid.shape, F32)
    temp = jnp.zeros(zid.shape, F32)
    for k in range(htc.shape[0]):
        coef = jnp.where(zid == k, htc[k], coef)
        temp = jnp.where(zid == k, gas[0, k], temp)
    for tab, values in ((coef_tab, coef), (temp_tab, temp)):
        rows_tab[...] = jnp.zeros_like(rows_tab)
        for z in range(nz):
            rows_tab[2 * z : 2 * z + 1, :] = values[z : z + 1, :]
            at = (2 * z - 1) % ny
            rows_tab[at : at + 1, :] = values[nz + z : nz + z + 1, :]
        tab[...] = rows_tab[...].T
    iyt[...] = inv_y[...].astype(F32).T.astype(BF16)

    row = lax.broadcasted_iota(jnp.int32, (nx, ny), 0)
    lane = lax.broadcasted_iota(jnp.int32, (nx, ny), 1)

    def conductivity(v):
        return 0.5 + 0.25 * jnp.tanh(v)

    def edges(v):
        v[0] = jnp.where(s > 0, v[0], 0.0)
        v[nz + 1] = jnp.where(s < S - 1, v[nz + 1], 0.0)
        q[0] = conductivity(v[0])
        q[nz + 1] = conductivity(v[nz + 1])

    def solved(v, z):
        c, qc = v[z + 1], q[z + 1]
        outer = (qc + 0.5) * c
        flux = (q[z + 2] + qc) * (v[z + 2] - c) - (q[z] + qc) * (c - v[z])
        for axis, index, last in ((0, row, nx - 1), (1, lane, ny - 1)):
            n = c.shape[axis]
            vn, qn = pltpu.roll(c, n - 1, axis), pltpu.roll(qc, n - 1, axis)
            ahead = jnp.where(index == last, -outer, (qn + qc) * (vn - c))
            behind = jnp.where(index == 0, outer, pltpu.roll(ahead, 1, axis))
            flux = flux + ahead - behind
        turn = lax.rem(ny - 2 * z, ny)
        face_coef = pltpu.roll(coef_tab[...], turn, 1)
        face_temp = pltpu.roll(temp_tab[...], turn, 1)
        on_face = (lane == 0) | (lane == ny - 1)
        surface = jnp.where(on_face, face_coef * (face_temp - c), 0.0)
        cooled = COOLING * holes[z].astype(F32) * (COOLANT - c)
        e = (TIME_STEP * (flux + surface + cooled)).astype(BF16)
        x = jnp.dot(inv_x[...], e, preferred_element_type=F32).astype(BF16)
        return c, jnp.dot(x, iyt[...], preferred_element_type=F32)

    def coded(v):
        top = jnp.max(jnp.abs(v), axis=0, keepdims=True)
        unit = jnp.maximum(top, 1e-30) * (1.0 / 32767.0)
        steps = jnp.round(v * (1.0 / unit))
        return steps.astype(jnp.int32).astype(jnp.int16), unit

    def decoded(steps, unit):
        return steps.astype(jnp.int32).astype(F32) * unit

    def own_copy(i):
        field = u[i]
        va[i + 1] = field
        q[i + 1] = conductivity(field)

    loop(nz, own_copy)

    def keep(z, p):
        planar[z] = p
        turned[pl.ds(z, nx, stride=nz), :] = p

    def first(i):
        z = 1 + 2 * i
        _, p = solved(va, z)
        _, r = solved(va, z + 1)
        keep(z, p)
        keep(z + 1, r)

    loop((nz - 2) // 2, first)
    halo[0].wait_recv()
    halo[1].wait_recv()
    edges(va)
    p, r = solved(va, 0)[1], solved(va, nz - 1)[1]
    keep(0, p)
    keep(nz - 1, r)

    def c_copy(k):
        to = lax.rem(s + 1 + k, S)
        return remote(
            cs.at[pl.ds(to * xb, xb)], cr.at[s], c_s.at[to], c_r.at[s], t, to
        )

    def c_block(to):
        block = turned[pl.ds(to * blk, blk), :]
        return block.reshape(xb, nz, ny).astype(BF16)

    def c_send(k):
        to = lax.rem(s + 1 + k, S)
        cs[pl.ds(to * xb, xb)] = c_block(to)
        c_copy(k).start()

    loop(S - 1, c_send)
    cr[s] = c_block(s)

    def decay(m, speed):
        return m[0:1, :] * jnp.exp(-(speed * m[1:2, :]))

    def lines(ref, k):
        return ref[:, pl.ds(pl.multiple_of(k * xb, xb), xb), :].reshape(blk, ny)

    def base(k):
        field = lines(u, k)
        aff[k] = field - decay(meta, lines(rate, k)) * field

    loop(S, base)
    mates.wait_recv()
    low = jnp.where(core == 0, meta[...], meta_pt[...])
    high = jnp.where(core == 0, meta_pt[...], meta[...])

    def c_wait(k):
        frm = lax.rem(s + 1 + k, S)
        remote(cs.at[pl.ds(0, xb)], cr.at[frm], c_s.at[frm], c_r.at[frm], t, frm).wait_recv()

    loop(S - 1, c_wait)
    for x in range(xb):
        es[pl.ds(x, S * nz, stride=xb), :] = jnp.dot(
            inv_z[...], cr[:, x].reshape(S * nz, ny), preferred_element_type=F32
        )

    def solution_of(k):
        return es[pl.ds(pl.multiple_of(k * blk, blk), blk), :]

    def e_copies(to):
        return (
            remote(eq.at[to], er_q.at[s], e_s.at[to], e_r.at[s], t, to),
            remote(eu.at[to], er_u.at[s], e_s.at[S + to], e_r.at[S + s], t, to),
        )

    def e_send(k):
        to = lax.rem(s + 1 + k, S)
        eq[to], eu[to] = coded(solution_of(to))
        for c in e_copies(to):
            c.start()

    loop(S - 1, e_send)

    def swap(k):
        return remote(
            aff.at[k], px.at[lax.rem(k, H)],
            swap_s.at[lax.rem(k, H)], swap_r.at[lax.rem(k, H)], mate, s,
        )

    def g_copies(to):
        there = 2 * to + core
        return (
            remote(gs_q.at[to], gr_q.at[chip], g_s.at[to], g_r.at[chip], there, s),
            remote(gs_u.at[to], gr_u.at[chip], g_s.at[M + to], g_r.at[M + chip], there, s),
        )

    def maps(k, rows):
        own, other = aff[k, rows, :], px[lax.rem(k, H), rows, :]
        return jnp.where(core == 0, own, other), jnp.where(core == 0, other, own)

    def take(frm, part):
        ver[frm] = part
        aff[frm] = aff[frm] + part

        @pl.when(frm // H != core)
        def _():
            swap(frm).start()

    def e_take(k):
        frm = lax.rem(s + S - 1 - k, S)
        remote(eq.at[0], er_q.at[frm], e_s.at[frm], e_r.at[frm], t, frm).wait_recv()
        remote(eu.at[0], er_u.at[frm], e_s.at[frm], e_r.at[S + frm], t, frm).wait_recv()
        take(frm, decoded(er_q[frm], er_u[frm]))

    def composed(k):
        frm = lax.rem(s + S - k, S)

        @pl.when(frm // H == core)
        def _():
            swap(frm).wait_recv()
            speed = lines(rate, frm)
            for r in range(ratio):
                block = lax.rem(frm, H) * ratio + r
                lo, hi = maps(frm, slice(r * rb, r * rb + rb))
                steps, unit = coded(decay(high, speed[r * rb : r * rb + rb]) * lo + hi)
                gs_q[block] = steps
                gs_u[block] = jnp.concatenate(
                    [low[0:1] * high[0:1], low[1:2] + high[1:2], unit, unit], axis=0
                )

                @pl.when(block != chip)
                def _():
                    for c in g_copies(block):
                        c.start()

    take(s, solution_of(s))
    e_take(0)

    def stream(k):
        e_take(k + 1)
        composed(k)

    loop(S - 2, stream)
    composed(S - 2)
    composed(S - 1)
    gr_q[chip] = gs_q[chip]
    gr_u[chip] = gs_u[chip]

    def plane(ref, z):
        return ref[:, pl.ds(pl.multiple_of(z * xb, xb), xb), :]

    def defect(z):
        rows = pl.ds(pl.multiple_of(z * xb, xb), xb)
        ver[:, rows, :] = ver[:, rows, :] - planar[z].reshape(S, xb, ny)

    loop(nz, defect)

    def cells(ref, block):
        k, r = core * H + block // ratio, lax.rem(block, ratio)
        return ref.at[pl.ds(r * zr, zr), pl.ds(pl.multiple_of(k * xb, xb), xb)]

    def i_copies(to):
        there = 2 * to + core
        return (
            remote(is_q.at[to], ir_q.at[chip], i_s.at[to], i_r.at[chip], there, s),
            remote(is_u.at[to], ir_u.at[chip], i_s.at[M + to], i_r.at[M + chip], there, s),
        )

    speed = cells(rate, chip)[...].reshape(rb, ny)

    def close(m, carry):
        total, kept, length = carry

        @pl.when(m != chip)
        def _():
            there = 2 * m + core
            remote(gs_q.at[0], gr_q.at[m], g_s.at[m], g_r.at[m], there, s).wait_recv()
            remote(gs_u.at[0], gr_u.at[m], g_s.at[m], g_r.at[M + m], there, s).wait_recv()

        h, d = gr_u[m, 0:1], gr_u[m, 1:2]
        factor = h * jnp.exp(-(speed * d))
        term = decoded(gr_q[m], gr_u[m, 2:3])
        jm[m] = factor
        gf[m] = term
        return factor * total + term, kept * h, length + d

    total, kept, length = lax.fori_loop(
        0, M, close,
        (jnp.zeros((rb, ny), F32), jnp.ones((1, ny), F32), jnp.zeros((1, ny), F32)),
    )

    def march(m, state):
        is_q[m], is_u[m] = coded(state)

        @pl.when(m != chip)
        def _():
            for c in i_copies(m):
                c.start()

        return jm[m] * state + gf[m]

    lax.fori_loop(0, M, march, total / (1.0 - kept * jnp.exp(-(speed * length))))

    def give(block):
        return remote(
            cells(ps, block), cells(vb.at[pl.ds(1, nz)], block),
            give_s.at[block], give_r.at[block], mate, s,
        )

    def predict(block, p0):
        k, r = core * H + block // ratio, lax.rem(block, ratio)
        lo, _ = maps(k, pl.ds(pl.multiple_of(r * rb, rb), rb))
        p1 = decay(low, cells(rate, block)[...].reshape(rb, ny)) * p0 + lo
        mine = jnp.where(core == 0, p0, p1).reshape(zr, xb, ny)
        there = (pl.ds(r * zr, zr), pl.ds(pl.multiple_of(k * xb, xb), xb))
        here = (pl.ds(1 + r * zr, zr), pl.ds(pl.multiple_of(k * xb, xb), xb))
        vb[here] = mine
        q[here] = conductivity(mine)
        ps[there] = jnp.where(core == 0, p1, p0).reshape(zr, xb, ny)
        give(block).start()

    predict(chip, decoded(is_q[chip], is_u[chip]))

    def i_take(k):
        frm = lax.rem(chip + 1 + k, M)
        there = 2 * frm + core
        remote(is_q.at[0], ir_q.at[frm], i_s.at[frm], i_r.at[frm], there, s).wait_recv()
        remote(is_u.at[0], ir_u.at[frm], i_s.at[frm], i_r.at[M + frm], there, s).wait_recv()
        predict(frm, decoded(ir_q[frm], ir_u[frm]))

    loop(M - 1, i_take)
    xs = pl.ds(pl.multiple_of(base_x, nx // 2), nx // 2)
    hb = []
    for i, (src, z, side, to) in enumerate(
        (
            (ps, 0, 1, down), (ps, nz - 1, 0, up), (vb, 1, 1, down), (vb, nz, 0, up),
        )
    ):
        hb.append(
            remote(
                src.at[z, xs], vb.at[side * (nz + 1), xs],
                hb_s.at[i], hb_r.at[2 * side + core], mate if i < 2 else t, to,
            )
        )
    for c in hb:
        c.start()

    def give_take(k):
        frm = lax.rem(chip + k, M)
        x = (1 - core) * H + frm // ratio
        where = (pl.ds(1 + lax.rem(frm, ratio) * zr, zr), pl.ds(pl.multiple_of(x * xb, xb), xb))
        remote(cells(ps, frm), vb.at[where], give_s.at[frm], give_r.at[frm], mate, s).wait_recv()
        q[where] = conductivity(vb[where])

    loop(M, give_take)

    def o_copies(z):
        return (
            remote(oq.at[z], out_q.at[z], o_s.at[z], o_r.at[z], nt, s),
            remote(ou.at[z], out_u.at[z], o_s.at[nz + z], o_r.at[nz + z], nt, s),
        )

    def second(z0, z1):
        c0, p = solved(vb, z0)
        c1, r = solved(vb, z1)
        oq[z0], ou[z0] = coded(c0 + p + plane(ver, z0).reshape(nx, ny))
        oq[z1], ou[z1] = coded(c1 + r + plane(ver, z1).reshape(nx, ny))
        for c in o_copies(z0) + o_copies(z1):
            c.start()

    loop((nz - 2) // 2, lambda i: second(1 + 2 * i, 2 + 2 * i))
    for side in range(2):
        for c in range(2):
            remote(
                ps.at[0, xs], vb.at[side * (nz + 1), pl.ds(c * (nx // 2), nx // 2)],
                hb_s.at[0], hb_r.at[2 * side + c], t, down,
            ).wait_recv()
    edges(vb)
    second(0, nz - 1)

    def sent(copies):
        for c in copies:
            c.wait_send()

    sent(halo + [mates] + hb)
    loop(S - 1, lambda k: c_copy(k).wait_send())
    loop(S - 1, lambda k: sent(e_copies(lax.rem(s + 1 + k, S))))
    loop(H, lambda k: swap((1 - core) * H + k).wait_send())
    loop(M - 1, lambda k: sent(g_copies(lax.rem(chip + 1 + k, M))))
    loop(M - 1, lambda k: sent(i_copies(lax.rem(chip + 1 + k, M))))
    loop(M, lambda k: give(k).wait_send())

    def arrived(z):
        for c in o_copies(z):
            c.wait()

    loop(nz, arrived)


def per_device(T, S, starts, holes, rate, zones, htc, gas, hold, duration, inv_x, inv_y, inv_z):
    _, nz, nx, ny = starts.shape
    xb, M = nx // S, T // 2
    blk, rb = nz * xb, nz * nx // 2 // M
    hbm = pl.BlockSpec(memory_space=pltpu.HBM)
    smem = pl.BlockSpec(memory_space=pltpu.SMEM)
    dma = lambda n: pltpu.SemaphoreType.DMA((n,))
    i16 = lambda *shape: pltpu.VMEM(shape, jnp.int16)
    v32 = lambda *shape: pltpu.VMEM(shape, F32)
    steps, unit = pl.pallas_call(
        functools.partial(kernel, T, S),
        out_shape=(
            jax.ShapeDtypeStruct((nz, nx, ny), jnp.int16),
            jax.ShapeDtypeStruct((nz, 1, ny), F32),
        ),
        in_specs=[hbm, hbm, hbm, hbm, smem, smem, smem, smem, hbm, hbm, hbm],
        out_specs=(hbm, hbm),
        scratch_shapes=[
            v32(nz, nx, ny), pltpu.VMEM((nz, nx, ny), jnp.int32), v32(nz, nx, ny),
            pltpu.VMEM((2 * nz, nx), jnp.int32), pltpu.VMEM((nx, nx), BF16),
            pltpu.VMEM((ny, ny), BF16), pltpu.VMEM((S * nz, S * nz), BF16), dma(7),
            v32(nz + 2, nx, ny), v32(nz + 2, nx, ny), v32(nz + 2, nx, ny),
            pltpu.VMEM((ny, ny), BF16),
            v32(ny, nx), v32(nx, ny), v32(nx, ny),
            v32(8, ny), v32(8, ny),
            v32(nz, nx, ny), v32(nx * nz, ny),
            pltpu.VMEM((nx, nz, ny), BF16), pltpu.VMEM((S, xb, nz, ny), BF16),
            v32(S * blk, ny), v32(S, blk, ny), v32(S // 2, blk, ny),
            v32(S, blk, ny), v32(nz, nx, ny),
            v32(M, rb, ny), v32(M, rb, ny),
            i16(S, blk, ny), v32(S, 1, ny), i16(S, blk, ny), v32(S, 1, ny),
            i16(M, rb, ny), v32(M, 4, ny), i16(M, rb, ny), v32(M, 4, ny),
            i16(M, rb, ny), v32(M, 1, ny), i16(M, rb, ny), v32(M, 1, ny),
            i16(nz, nx, ny), v32(nz, 1, ny),
            dma(2), dma(2), dma(1), dma(1), dma(S), dma(S), dma(2 * S), dma(2 * S),
            dma(S // 2), dma(S // 2),
            dma(2 * M), dma(2 * M), dma(2 * M), dma(2 * M), dma(M), dma(M), dma(4), dma(4),
            dma(2 * nz), dma(2 * nz),
        ],
        compiler_params=pltpu.CompilerParams(
            collective_id=0, has_side_effects=True, vmem_limit_bytes=60 * 1024 * 1024
        ),
    )(
        starts[0], holes, rate, zones.reshape(2 * nz, nx),
        htc, gas, hold, duration, inv_x, inv_y, inv_z,
    )
    return (steps.astype(F32) * unit)[None]


def solution(mesh):
    return jax.shard_map(
        functools.partial(per_device, mesh.shape["tm"], mesh.shape["space"]),
        mesh=mesh,
        in_specs=(
            P("tm", "space", None, None),
            P("space", None, None),
            P("space", None, None),
            P(None, "space", None),
            P(),
            P("tm", None),
            P("tm"),
            P("tm"),
            P(),
            P(),
            P(),
        ),
        out_specs=P("tm", "space", None, None),
        check_vma=False,
    )
```

```python
import functools

import jax
import jax.numpy as jnp
from jax import lax
from jax.experimental import pallas as pl
from jax.experimental.pallas import tpu as pltpu
from jax.sharding import PartitionSpec as P

COOLING = 4.0
COOLANT = -1.0
TIME_STEP = 0.2
MESH = pl.DeviceIdType.MESH
F32 = jnp.float32
BF16 = jnp.bfloat16


def loop(count, body):
    lax.fori_loop(0, count, lambda i, c: (body(i), c)[1], 0)


def grouped(count, body):
    width = next(w for w in (4, 3, 2, 1) if count % w == 0)
    loop(count // width, lambda g: body([g * width + i for i in range(width)]))


def kernel(
    T, S,
    u_in, holes_in, rate_in, zones_in, htc, gas, hold, duration, inv_x_in, inv_y_in, inv_z_in,
    out_q, out_u,
    u, holes, rate, zones, inv_x, inv_y, inv_z, load_s,
    va, vb, q, iyt, rows_tab, coef_tab, temp_tab, meta, meta_pt,
    planar, turned, cs, cr, es, aff, px, ver, ps, jm, gf, states,
    eq, eu, er_q, er_u, gs_q, gs_u, gr_q, gr_u, is_q, is_u, ir_q, ir_u, oq, ou,
    halo_s, halo_r, meta_s, meta_r, c_s, c_r, e_s, e_r, swap_s, swap_r,
    g_s, g_r, i_s, i_r, give_s, give_r, hb_s, hb_r, o_s, o_r,
):
    t, s = lax.axis_index("tm"), lax.axis_index("space")
    core = lax.rem(t, 2)
    chip = t // 2
    M, H = T // 2, S // 2
    mate = t + 1 - 2 * core
    nt, pt = lax.rem(t + 1, T), lax.rem(t + T - 1, T)
    down, up = lax.rem(s + S - 1, S), lax.rem(s + 1, S)
    nz, nx, ny = u.shape
    xb = nx // S
    blk = nz * xb
    rb = nz * nx // 2 // M
    zr = rb // xb
    ratio = blk // rb
    base_x = core * (nx // 2)

    def remote(src, dst, send, recv, tt, ss):
        return pltpu.make_async_remote_copy(
            src_ref=src, dst_ref=dst, send_sem=send, recv_sem=recv,
            device_id=(tt, ss), device_id_type=MESH,
        )

    loads = [
        pltpu.make_async_copy(src, dst, load_s.at[i])
        for i, (src, dst) in enumerate(
            (
                (u_in, u), (zones_in, zones), (inv_y_in, inv_y), (inv_x_in, inv_x),
                (holes_in, holes), (rate_in, rate), (inv_z_in, inv_z),
            )
        )
    ]
    for c in loads:
        c.start()

    barrier = pltpu.get_barrier_semaphore()

    def greet(tt, ss):
        pl.semaphore_signal(barrier, inc=1, device_id=(tt, ss), device_id_type=MESH)

    loop(S - 1, lambda k: greet(t, lax.rem(s + 1 + k, S)))
    loop(M - 1, lambda k: greet(2 * lax.rem(chip + 1 + k, M) + core, s))
    greet(mate, s)
    greet(mate, down)
    greet(mate, up)
    greet(pt, s)
    loads[0].wait()
    pl.semaphore_wait(barrier, S - 1 + M - 1 + 4)

    halo = [
        remote(u.at[nz - 1], va.at[0], halo_s.at[0], halo_r.at[0], t, up),
        remote(u.at[0], va.at[nz + 1], halo_s.at[1], halo_r.at[1], t, down),
    ]
    for c in halo:
        c.start()
    meta[0:1, :] = jnp.full((1, ny), hold[0], F32)
    meta[1:2, :] = jnp.full((1, ny), duration[0] * (1.0 / T), F32)
    meta[2:8, :] = jnp.zeros((6, ny), F32)
    mates = remote(meta, meta_pt, meta_s.at[0], meta_r.at[0], mate, s)
    mates.start()

    for c in loads[1:]:
        c.wait()
    zid = zones[...]
    coef = jnp.zeros(zid.shape, F32)
    temp = jnp.zeros(zid.shape, F32)
    for k in range(htc.shape[0]):
        coef = jnp.where(zid == k, htc[k], coef)
        temp = jnp.where(zid == k, gas[0, k], temp)
    for tab, values in ((coef_tab, coef), (temp_tab, temp)):
        rows_tab[...] = jnp.zeros_like(rows_tab)
        for z in range(nz):
            rows_tab[2 * z : 2 * z + 1, :] = values[z : z + 1, :]
            at = (2 * z - 1) % ny
            rows_tab[at : at + 1, :] = values[nz + z : nz + z + 1, :]
        tab[...] = rows_tab[...].T
    iyt[...] = inv_y[...].astype(F32).T.astype(BF16)

    row = lax.broadcasted_iota(jnp.int32, (nx, ny), 0)
    lane = lax.broadcasted_iota(jnp.int32, (nx, ny), 1)

    def conductivity(v):
        return 0.5 + 0.25 * jnp.tanh(v)

    def edges(v):
        v[0] = jnp.where(s > 0, v[0], 0.0)
        v[nz + 1] = jnp.where(s < S - 1, v[nz + 1], 0.0)
        q[0] = conductivity(v[0])
        q[nz + 1] = conductivity(v[nz + 1])

    def solved(v, z):
        c, qc = v[z + 1], q[z + 1]
        outer = (qc + 0.5) * c
        flux = (q[z + 2] + qc) * (v[z + 2] - c) - (q[z] + qc) * (c - v[z])
        for axis, index, last in ((0, row, nx - 1), (1, lane, ny - 1)):
            n = c.shape[axis]
            vn, qn = pltpu.roll(c, n - 1, axis), pltpu.roll(qc, n - 1, axis)
            ahead = jnp.where(index == last, -outer, (qn + qc) * (vn - c))
            behind = jnp.where(index == 0, outer, pltpu.roll(ahead, 1, axis))
            flux = flux + ahead - behind
        turn = lax.rem(ny - 2 * z, ny)
        face_coef = pltpu.roll(coef_tab[...], turn, 1)
        face_temp = pltpu.roll(temp_tab[...], turn, 1)
        on_face = (lane == 0) | (lane == ny - 1)
        surface = jnp.where(on_face, face_coef * (face_temp - c), 0.0)
        cooled = COOLING * holes[z].astype(F32) * (COOLANT - c)
        e = (TIME_STEP * (flux + surface + cooled)).astype(BF16)
        x = jnp.dot(inv_x[...], e, preferred_element_type=F32).astype(BF16)
        return c, jnp.dot(x, iyt[...], preferred_element_type=F32)

    def coded(v):
        top = jnp.max(jnp.abs(v), axis=0, keepdims=True)
        unit = jnp.maximum(top, 1e-30) * (1.0 / 32767.0)
        steps = jnp.round(v * (1.0 / unit))
        return steps.astype(jnp.int32).astype(jnp.int16), unit

    def decoded(steps, unit):
        return steps.astype(jnp.int32).astype(F32) * unit

    def own_copy(i):
        field = u[i]
        va[i + 1] = field
        q[i + 1] = conductivity(field)

    loop(nz, own_copy)

    def keep(z, p):
        planar[z] = p
        turned[pl.ds(z, nx, stride=nz), :] = p

    def first(i):
        z = 1 + 2 * i
        _, p = solved(va, z)
        _, r = solved(va, z + 1)
        keep(z, p)
        keep(z + 1, r)

    loop((nz - 2) // 2, first)
    halo[0].wait_recv()
    halo[1].wait_recv()
    edges(va)
    p, r = solved(va, 0)[1], solved(va, nz - 1)[1]
    keep(0, p)
    keep(nz - 1, r)

    def c_copy(k):
        to = lax.rem(s + 1 + k, S)
        return remote(
            cs.at[pl.ds(to * xb, xb)], cr.at[s], c_s.at[to], c_r.at[s], t, to
        )

    def c_block(to):
        block = turned[pl.ds(to * blk, blk), :]
        return block.reshape(xb, nz, ny).astype(BF16)

    def c_send(ks):
        tos = [lax.rem(s + 1 + k, S) for k in ks]
        for to in tos:
            cs[pl.ds(to * xb, xb)] = c_block(to)
        for k in ks:
            c_copy(k).start()

    grouped(S - 1, c_send)
    cr[s] = c_block(s)

    def decay(m, speed):
        return m[0:1, :] * jnp.exp(-(speed * m[1:2, :]))

    def lines(ref, k):
        return ref[:, pl.ds(pl.multiple_of(k * xb, xb), xb), :].reshape(blk, ny)

    def base(k):
        field = lines(u, k)
        rest = field - decay(meta, lines(rate, k)) * field
        for r in range(ratio):
            aff[k, r] = rest[r * rb : r * rb + rb]

    loop(S, base)
    mates.wait_recv()
    low = jnp.where(core == 0, meta[...], meta_pt[...])
    high = jnp.where(core == 0, meta_pt[...], meta[...])

    def c_wait(k):
        frm = lax.rem(s + 1 + k, S)
        remote(cs.at[pl.ds(0, xb)], cr.at[frm], c_s.at[frm], c_r.at[frm], t, frm).wait_recv()

    loop(S - 1, c_wait)
    for x in range(xb):
        es[pl.ds(x, S * nz, stride=xb), :] = jnp.dot(
            inv_z[...], cr[:, x].reshape(S * nz, ny), preferred_element_type=F32
        )

    def e_copies(to, r):
        i, j = to * ratio + r, s * ratio + r
        return (
            remote(eq.at[to, r], er_q.at[s, r], e_s.at[i], e_r.at[j], t, to),
            remote(
                eu.at[to, r], er_u.at[s, r], e_s.at[S * ratio + i], e_r.at[S * ratio + j], t, to
            ),
        )

    def start(copies):
        for c in copies:
            c.start()

    def e_send(r):
        def body(ks):
            tos = [lax.rem(s + 1 + k, S) for k in ks]
            codes = [
                coded(es[pl.ds(pl.multiple_of(to * blk + r * rb, rb), rb), :]) for to in tos
            ]
            for to, (steps, unit) in zip(tos, codes):
                eq[to, r], eu[to, r] = steps, unit
            for to in tos:
                pl.when(to != s)(lambda to=to: start(e_copies(to, r)))

        grouped(S, body)
        er_q[s, r], er_u[s, r] = eq[s, r], eu[s, r]

    for r in range(ratio):
        e_send(r)

    def swap(j, r):
        i = j * ratio + r
        return remote(
            aff.at[(1 - core) * H + j, r], px.at[j, r], swap_s.at[i], swap_r.at[i], mate, s
        )

    def g_copies(to):
        there = 2 * to + core
        return (
            remote(gs_q.at[to], gr_q.at[chip], g_s.at[to], g_r.at[chip], there, s),
            remote(gs_u.at[to], gr_u.at[chip], g_s.at[M + to], g_r.at[M + chip], there, s),
        )

    def maps(j, r):
        own, other = aff[core * H + j, r], px[j, r]
        return jnp.where(core == 0, own, other), jnp.where(core == 0, other, own)

    def e_take(r):
        def body(ks):
            frms = [lax.rem(s + S - k, S) for k in ks]
            for frm in frms:

                @pl.when(frm != s)
                def _():
                    i = frm * ratio + r
                    remote(
                        eq.at[0, r], er_q.at[frm, r], e_s.at[i], e_r.at[i], t, frm
                    ).wait_recv()
                    remote(
                        eu.at[0, r], er_u.at[frm, r], e_s.at[i], e_r.at[S * ratio + i], t, frm
                    ).wait_recv()

            parts = [decoded(er_q[frm, r], er_u[frm, r]) for frm in frms]
            sums = [aff[frm, r] + part for frm, part in zip(frms, parts)]
            for frm, part, total in zip(frms, parts, sums):
                ver[frm, r] = part
                aff[frm, r] = total
            for frm in frms:
                pl.when(frm // H != core)(lambda frm=frm: swap(lax.rem(frm, H), r).start())

        grouped(S, body)

    def cells(ref, block):
        k, r = core * H + block // ratio, lax.rem(block, ratio)
        return ref.at[pl.ds(r * zr, zr), pl.ds(pl.multiple_of(k * xb, xb), xb)]

    def compose(r):
        loop(H, lambda j: swap(j, r).wait_recv())

        def body(js):
            js = [lax.rem(chip // ratio + 1 + j, H) for j in js]
            codes = []
            for j in js:
                lo, hi = maps(j, r)
                speed = cells(rate, j * ratio + r)[...].reshape(rb, ny)
                codes.append(coded(decay(high, speed) * lo + hi))
            for j, (steps, unit) in zip(js, codes):
                gs_q[j * ratio + r] = steps
                gs_u[j * ratio + r] = jnp.concatenate(
                    [low[0:1] * high[0:1], low[1:2] + high[1:2], unit, unit], axis=0
                )
            for j in js:
                block = j * ratio + r
                pl.when(block != chip)(lambda block=block: start(g_copies(block)))

        grouped(H, body)

    def defect(r):
        def body(z):
            rows = pl.ds(pl.multiple_of(z * xb, xb), xb)
            ver[:, r, rows, :] = ver[:, r, rows, :] - planar[r * zr + z].reshape(S, xb, ny)

        loop(zr, body)

    def i_copies(to):
        there = 2 * to + core
        return (
            remote(is_q.at[to], ir_q.at[chip], i_s.at[to], i_r.at[chip], there, s),
            remote(is_u.at[to], ir_u.at[chip], i_s.at[M + to], i_r.at[M + chip], there, s),
        )

    def scan():
        gr_q[chip] = gs_q[chip]
        gr_u[chip] = gs_u[chip]
        speed = cells(rate, chip)[...].reshape(rb, ny)

        def arrive(ks):
            ms = [lax.rem(chip + k, M) for k in ks]
            for m in ms:

                @pl.when(m != chip)
                def _():
                    there = 2 * m + core
                    remote(gs_q.at[0], gr_q.at[m], g_s.at[m], g_r.at[m], there, s).wait_recv()
                    remote(
                        gs_u.at[0], gr_u.at[m], g_s.at[m], g_r.at[M + m], there, s
                    ).wait_recv()

            pairs = [
                (
                    gr_u[m, 0:1] * jnp.exp(-(speed * gr_u[m, 1:2])),
                    decoded(gr_q[m], gr_u[m, 2:3]),
                )
                for m in ms
            ]
            for m, (factor, term) in zip(ms, pairs):
                jm[m], gf[m] = factor, term

        grouped(M, arrive)
        total = gf[0]
        kept, length = gr_u[0, 0:1], gr_u[0, 1:2]
        for m in range(1, M):
            total = jm[m] * total + gf[m]
            kept, length = kept * gr_u[m, 0:1], length + gr_u[m, 1:2]
        state = total / (1.0 - kept * jnp.exp(-(speed * length)))
        for m in range(M):
            following = jm[m] * state + gf[m]
            states[m] = state
            state = following

        def leave(ks):
            ms = [lax.rem(chip + 1 + k, M) for k in ks]
            codes = [coded(states[m]) for m in ms]
            for m, (steps, unit) in zip(ms, codes):
                is_q[m], is_u[m] = steps, unit
            for m in ms:
                pl.when(m != chip)(lambda m=m: start(i_copies(m)))

        grouped(M, leave)
        ir_q[chip] = is_q[chip]
        ir_u[chip] = is_u[chip]

    for r in range(ratio):
        e_take(r)
        compose(r)
        defect(r)
        pl.when(lax.rem(chip, ratio) == r)(scan)

    def give(block):
        return remote(
            cells(ps, block), cells(vb.at[pl.ds(1, nz)], block),
            give_s.at[block], give_r.at[block], mate, s,
        )

    def i_take(r):
        def body(js):
            js = [lax.rem(chip // ratio + j, H) for j in js]
            blocks = [j * ratio + r for j in js]
            for frm in blocks:

                @pl.when(frm != chip)
                def _():
                    there = 2 * frm + core
                    remote(
                        is_q.at[0], ir_q.at[frm], i_s.at[frm], i_r.at[frm], there, s
                    ).wait_recv()
                    remote(
                        is_u.at[0], ir_u.at[frm], i_s.at[frm], i_r.at[M + frm], there, s
                    ).wait_recv()

            fields = []
            for j, block in zip(js, blocks):
                lo, _ = maps(j, r)
                p0 = decoded(ir_q[block], ir_u[block])
                p1 = decay(low, cells(rate, block)[...].reshape(rb, ny)) * p0 + lo
                mine = jnp.where(core == 0, p0, p1).reshape(zr, xb, ny)
                theirs = jnp.where(core == 0, p1, p0).reshape(zr, xb, ny)
                fields.append((mine, theirs, conductivity(mine)))
            for block, (mine, theirs, cond) in zip(blocks, fields):
                cells(ps, block)[...] = theirs
                cells(vb.at[pl.ds(1, nz)], block)[...] = mine
                cells(q.at[pl.ds(1, nz)], block)[...] = cond
            for block in blocks:
                give(block).start()

        grouped(H, body)

    xs = pl.ds(pl.multiple_of(base_x, nx // 2), nx // 2)
    hb = [
        remote(
            src.at[z, xs], vb.at[side * (nz + 1), xs],
            hb_s.at[i], hb_r.at[2 * side + core], mate if i % 2 == 0 else t, to,
        )
        for i, (src, z, side, to) in enumerate(
            ((ps, 0, 1, down), (vb, 1, 1, down), (ps, nz - 1, 0, up), (vb, nz, 0, up))
        )
    ]

    def give_take(r):
        def body(js):
            js = [lax.rem(chip // ratio + j, H) for j in js]
            places = []
            for j in js:
                block, x = j * ratio + r, (1 - core) * H + j
                where = (pl.ds(1 + r * zr, zr), pl.ds(pl.multiple_of(x * xb, xb), xb))
                remote(
                    cells(ps, block), vb.at[where], give_s.at[block], give_r.at[block], mate, s
                ).wait_recv()
                places.append(where)
            conds = [conductivity(vb[where]) for where in places]
            for where, cond in zip(places, conds):
                q[where] = cond

        grouped(H, body)

    def o_copies(z):
        return (
            remote(oq.at[z], out_q.at[z], o_s.at[z], o_r.at[z], nt, s),
            remote(ou.at[z], out_u.at[z], o_s.at[nz + z], o_r.at[nz + z], nt, s),
        )

    def plane(z):
        rows = pl.ds(pl.multiple_of(lax.rem(z, zr) * xb, xb), xb)
        return ver[:, z // zr, rows, :].reshape(nx, ny)

    def second(z0, z1):
        c0, p = solved(vb, z0)
        c1, r = solved(vb, z1)
        first_code = coded(c0 + p + plane(z0))
        second_code = coded(c1 + r + plane(z1))
        oq[z0], ou[z0] = first_code
        oq[z1], ou[z1] = second_code
        for c in o_copies(z0) + o_copies(z1):
            c.start()

    for r in range(ratio):
        i_take(r)
        if r == 0:
            start(hb[:2])
        if r == ratio - 1:
            start(hb[2:])
        give_take(r)
        z0 = max(1, r * zr - 1)
        pairs = ((r + 1) * zr - 1 - z0) // 2
        loop(pairs, lambda i, z0=z0: second(z0 + 2 * i, z0 + 1 + 2 * i))
    for side in range(2):
        for c in range(2):
            remote(
                ps.at[0, xs], vb.at[side * (nz + 1), pl.ds(c * (nx // 2), nx // 2)],
                hb_s.at[0], hb_r.at[2 * side + c], t, down,
            ).wait_recv()
    edges(vb)
    second(0, nz - 1)

    def sent(copies):
        for c in copies:
            c.wait_send()

    sent(halo + [mates] + hb)
    loop(S - 1, lambda k: c_copy(k).wait_send())
    for r in range(ratio):
        loop(S - 1, lambda k, r=r: sent(e_copies(lax.rem(s + 1 + k, S), r)))
        loop(H, lambda j, r=r: swap(j, r).wait_send())
    loop(M - 1, lambda k: sent(g_copies(lax.rem(chip + 1 + k, M))))
    loop(M - 1, lambda k: sent(i_copies(lax.rem(chip + 1 + k, M))))
    loop(M, lambda k: give(k).wait_send())

    def arrived(z):
        for c in o_copies(z):
            c.wait()

    loop(nz, arrived)


def per_device(T, S, starts, holes, rate, zones, htc, gas, hold, duration, inv_x, inv_y, inv_z):
    _, nz, nx, ny = starts.shape
    xb, M = nx // S, T // 2
    blk, rb = nz * xb, nz * nx // 2 // M
    ratio = blk // rb
    hbm = pl.BlockSpec(memory_space=pltpu.HBM)
    smem = pl.BlockSpec(memory_space=pltpu.SMEM)
    dma = lambda n: pltpu.SemaphoreType.DMA((n,))
    i16 = lambda *shape: pltpu.VMEM(shape, jnp.int16)
    v32 = lambda *shape: pltpu.VMEM(shape, F32)
    steps, unit = pl.pallas_call(
        functools.partial(kernel, T, S),
        out_shape=(
            jax.ShapeDtypeStruct((nz, nx, ny), jnp.int16),
            jax.ShapeDtypeStruct((nz, 1, ny), F32),
        ),
        in_specs=[hbm, hbm, hbm, hbm, smem, smem, smem, smem, hbm, hbm, hbm],
        out_specs=(hbm, hbm),
        scratch_shapes=[
            v32(nz, nx, ny), pltpu.VMEM((nz, nx, ny), jnp.int32), v32(nz, nx, ny),
            pltpu.VMEM((2 * nz, nx), jnp.int32), pltpu.VMEM((nx, nx), BF16),
            pltpu.VMEM((ny, ny), BF16), pltpu.VMEM((S * nz, S * nz), BF16), dma(7),
            v32(nz + 2, nx, ny), v32(nz + 2, nx, ny), v32(nz + 2, nx, ny),
            pltpu.VMEM((ny, ny), BF16),
            v32(ny, nx), v32(nx, ny), v32(nx, ny),
            v32(8, ny), v32(8, ny),
            v32(nz, nx, ny), v32(nx * nz, ny),
            pltpu.VMEM((nx, nz, ny), BF16), pltpu.VMEM((S, xb, nz, ny), BF16),
            v32(S * blk, ny), v32(S, ratio, rb, ny), v32(S // 2, ratio, rb, ny),
            v32(S, ratio, rb, ny), v32(nz, nx, ny),
            v32(M, rb, ny), v32(M, rb, ny), v32(M, rb, ny),
            i16(S, ratio, rb, ny), v32(S, ratio, 1, ny),
            i16(S, ratio, rb, ny), v32(S, ratio, 1, ny),
            i16(M, rb, ny), v32(M, 4, ny), i16(M, rb, ny), v32(M, 4, ny),
            i16(M, rb, ny), v32(M, 1, ny), i16(M, rb, ny), v32(M, 1, ny),
            i16(nz, nx, ny), v32(nz, 1, ny),
            dma(2), dma(2), dma(1), dma(1), dma(S), dma(S),
            dma(2 * S * ratio), dma(2 * S * ratio), dma(M), dma(M),
            dma(2 * M), dma(2 * M), dma(2 * M), dma(2 * M), dma(M), dma(M), dma(4), dma(4),
            dma(2 * nz), dma(2 * nz),
        ],
        compiler_params=pltpu.CompilerParams(
            collective_id=0, has_side_effects=True, vmem_limit_bytes=60 * 1024 * 1024
        ),
    )(
        starts[0], holes, rate, zones.reshape(2 * nz, nx),
        htc, gas, hold, duration, inv_x, inv_y, inv_z,
    )
    return (steps.astype(F32) * unit)[None]


def solution(mesh):
    return jax.shard_map(
        functools.partial(per_device, mesh.shape["tm"], mesh.shape["space"]),
        mesh=mesh,
        in_specs=(
            P("tm", "space", None, None),
            P("space", None, None),
            P("space", None, None),
            P(None, "space", None),
            P(),
            P("tm", None),
            P("tm"),
            P("tm"),
            P(),
            P(),
            P(),
        ),
        out_specs=P("tm", "space", None, None),
        check_vma=False,
    )
```

```python
import functools

import jax
import jax.numpy as jnp
from jax import lax
from jax.experimental import pallas as pl
from jax.experimental.pallas import tpu as pltpu
from jax.sharding import PartitionSpec as P

COOLING = 4.0
COOLANT = -1.0
TIME_STEP = 0.2
MESH = pl.DeviceIdType.MESH
F32 = jnp.float32
BF16 = jnp.bfloat16


def loop(count, body):
    lax.fori_loop(0, count, lambda i, c: (body(i), c)[1], 0)


def kernel(
    T, S,
    u_in, holes_in, rate_in, zones_in, htc, gas, hold, duration, inv_x_in, inv_y_in, inv_z_in,
    out_q, out_u,
    u, holes, rate, zones, inv_x, inv_y, inv_z, load_s,
    va, vb, q, iyt, rows_tab, coef_tab, temp_tab, meta, meta_pt,
    planar, turned, cs, cr, es, aff, px, ver, ps, jm, gf, states,
    eq, eu, er_q, er_u, gs_q, gs_u, gr_q, gr_u, is_q, is_u, ir_q, ir_u, oq, ou,
    halo_s, halo_r, meta_s, meta_r, c_s, c_r, e_s, e_r, swap_s, swap_r,
    g_s, g_r, i_s, i_r, give_s, give_r, hb_s, hb_r, o_s, o_r,
):
    t, s = lax.axis_index("tm"), lax.axis_index("space")
    core = lax.rem(t, 2)
    chip = t // 2
    M, H = T // 2, S // 2
    mate = t + 1 - 2 * core
    nt, pt = lax.rem(t + 1, T), lax.rem(t + T - 1, T)
    down, up = lax.rem(s + S - 1, S), lax.rem(s + 1, S)
    nz, nx, ny = u.shape
    xb = nx // S
    blk = nz * xb
    rb = nz * nx // 2 // M
    zr = rb // xb
    ratio = blk // rb
    base_x = core * (nx // 2)

    def remote(src, dst, send, recv, tt, ss):
        return pltpu.make_async_remote_copy(
            src_ref=src, dst_ref=dst, send_sem=send, recv_sem=recv,
            device_id=(tt, ss), device_id_type=MESH,
        )

    loads = [
        pltpu.make_async_copy(src, dst, load_s.at[i])
        for i, (src, dst) in enumerate(
            (
                (u_in, u), (zones_in, zones), (inv_y_in, inv_y), (inv_x_in, inv_x),
                (holes_in, holes), (rate_in, rate), (inv_z_in, inv_z),
            )
        )
    ]
    for c in loads:
        c.start()

    barrier = pltpu.get_barrier_semaphore()

    def greet(tt, ss):
        pl.semaphore_signal(barrier, inc=1, device_id=(tt, ss), device_id_type=MESH)

    loop(S - 1, lambda k: greet(t, lax.rem(s + 1 + k, S)))
    loop(M - 1, lambda k: greet(2 * lax.rem(chip + 1 + k, M) + core, s))
    greet(mate, s)
    greet(mate, down)
    greet(mate, up)
    greet(pt, s)
    loads[0].wait()
    pl.semaphore_wait(barrier, S - 1 + M - 1 + 4)

    halo = [
        remote(u.at[nz - 1], va.at[0], halo_s.at[0], halo_r.at[0], t, up),
        remote(u.at[0], va.at[nz + 1], halo_s.at[1], halo_r.at[1], t, down),
    ]
    for c in halo:
        c.start()
    meta[0:1, :] = jnp.full((1, ny), hold[0], F32)
    meta[1:2, :] = jnp.full((1, ny), duration[0] * (1.0 / T), F32)
    meta[2:8, :] = jnp.zeros((6, ny), F32)
    mates = remote(meta, meta_pt, meta_s.at[0], meta_r.at[0], mate, s)
    mates.start()

    for c in loads[1:]:
        c.wait()
    zid = zones[...]
    coef = jnp.zeros(zid.shape, F32)
    temp = jnp.zeros(zid.shape, F32)
    for k in range(htc.shape[0]):
        coef = jnp.where(zid == k, htc[k], coef)
        temp = jnp.where(zid == k, gas[0, k], temp)
    for tab, values in ((coef_tab, coef), (temp_tab, temp)):
        rows_tab[...] = jnp.zeros_like(rows_tab)
        for z in range(nz):
            rows_tab[2 * z : 2 * z + 1, :] = values[z : z + 1, :]
            at = (2 * z - 1) % ny
            rows_tab[at : at + 1, :] = values[nz + z : nz + z + 1, :]
        tab[...] = rows_tab[...].T
    iyt[...] = inv_y[...].astype(F32).T.astype(BF16)

    row = lax.broadcasted_iota(jnp.int32, (nx, ny), 0)
    lane = lax.broadcasted_iota(jnp.int32, (nx, ny), 1)

    def conductivity(v):
        return 0.5 + 0.25 * jnp.tanh(v)

    def edges(v):
        v[0] = jnp.where(s > 0, v[0], 0.0)
        v[nz + 1] = jnp.where(s < S - 1, v[nz + 1], 0.0)
        q[0] = conductivity(v[0])
        q[nz + 1] = conductivity(v[nz + 1])

    def solved(v, z):
        c, qc = v[z + 1], q[z + 1]
        outer = (qc + 0.5) * c
        flux = (q[z + 2] + qc) * (v[z + 2] - c) - (q[z] + qc) * (c - v[z])
        for axis, index, last in ((0, row, nx - 1), (1, lane, ny - 1)):
            n = c.shape[axis]
            vn, qn = pltpu.roll(c, n - 1, axis), pltpu.roll(qc, n - 1, axis)
            ahead = jnp.where(index == last, -outer, (qn + qc) * (vn - c))
            behind = jnp.where(index == 0, outer, pltpu.roll(ahead, 1, axis))
            flux = flux + ahead - behind
        turn = lax.rem(ny - 2 * z, ny)
        face_coef = pltpu.roll(coef_tab[...], turn, 1)
        face_temp = pltpu.roll(temp_tab[...], turn, 1)
        on_face = (lane == 0) | (lane == ny - 1)
        surface = jnp.where(on_face, face_coef * (face_temp - c), 0.0)
        cooled = COOLING * holes[z].astype(F32) * (COOLANT - c)
        e = (TIME_STEP * (flux + surface + cooled)).astype(BF16)
        x = jnp.dot(inv_x[...], e, preferred_element_type=F32).astype(BF16)
        return c, jnp.dot(x, iyt[...], preferred_element_type=F32)

    def coded(v):
        top = jnp.max(jnp.abs(v), axis=0, keepdims=True)
        unit = jnp.maximum(top, 1e-30) * (1.0 / 32767.0)
        steps = jnp.round(v * (1.0 / unit))
        return steps.astype(jnp.int32).astype(jnp.int16), unit

    def decoded(steps, unit):
        return steps.astype(jnp.int32).astype(F32) * unit

    def own_copy(i):
        field = u[i]
        va[i + 1] = field
        q[i + 1] = conductivity(field)

    loop(nz, own_copy)

    def keep(z, p):
        planar[z] = p
        turned[pl.ds(z, nx, stride=nz), :] = p

    def pair(i):
        return 1 + 2 * i, lax.rem(2 + 2 * i, nz)

    def first(i):
        @pl.when(i == nz // 2 - 1)
        def _():
            halo[0].wait_recv()
            halo[1].wait_recv()
            edges(va)

        z0, z1 = pair(i)
        _, p = solved(va, z0)
        _, r = solved(va, z1)
        keep(z0, p)
        keep(z1, r)

    loop(nz // 2, first)

    def stride(k, size=S):
        odd = lax.rem(k, 2)
        return (1 - odd) * (1 + k // 2) + odd * (size - 1 - k // 2)

    def to_of(k):
        return lax.rem(s + stride(k), S)

    def from_of(k):
        return lax.rem(s + S - stride(k), S)

    def c_copy(k):
        to = to_of(k)
        return remote(
            cs.at[pl.ds(to * xb, xb)], cr.at[s], c_s.at[to], c_r.at[s], t, to
        )

    def c_block(to):
        block = turned[pl.ds(to * blk, blk), :]
        return block.reshape(xb, nz, ny).astype(BF16)

    def c_send(k):
        to = to_of(k)
        cs[pl.ds(to * xb, xb)] = c_block(to)
        c_copy(k).start()

    loop(S - 1, c_send)
    cr[s] = c_block(s)

    def decay(m, speed):
        return m[0:1, :] * jnp.exp(-(speed * m[1:2, :]))

    def lines(ref, k):
        return ref[:, pl.ds(pl.multiple_of(k * xb, xb), xb), :].reshape(blk, ny)

    def base(k):
        field = lines(u, k)
        aff[k] = field - decay(meta, lines(rate, k)) * field

    loop(S, base)
    mates.wait_recv()
    low = jnp.where(core == 0, meta[...], meta_pt[...])
    high = jnp.where(core == 0, meta_pt[...], meta[...])

    def c_wait(k):
        frm = lax.rem(s + 1 + k, S)
        remote(cs.at[pl.ds(0, xb)], cr.at[frm], c_s.at[frm], c_r.at[frm], t, frm).wait_recv()

    loop(S - 1, c_wait)
    def solve(x):
        es[pl.ds(x, S * nz, stride=xb), :] = jnp.dot(
            inv_z[...], cr[:, x].reshape(S * nz, ny), preferred_element_type=F32
        )

    loop(xb, solve)

    def solution_of(k):
        return es[pl.ds(pl.multiple_of(k * blk, blk), blk), :]

    def e_copies(to):
        return (
            remote(eq.at[to], er_q.at[s], e_s.at[to], e_r.at[s], t, to),
            remote(eu.at[to], er_u.at[s], e_s.at[S + to], e_r.at[S + s], t, to),
        )

    def e_send(k):
        to = to_of(k)
        eq[to], eu[to] = coded(solution_of(to))
        for c in e_copies(to):
            c.start()

    loop(S - 1, e_send)

    def swap(k):
        return remote(
            aff.at[k], px.at[lax.rem(k, H)],
            swap_s.at[lax.rem(k, H)], swap_r.at[lax.rem(k, H)], mate, s,
        )

    def g_copies(to):
        there = 2 * to + core
        return (
            remote(gs_q.at[to], gr_q.at[chip], g_s.at[to], g_r.at[chip], there, s),
            remote(gs_u.at[to], gr_u.at[chip], g_s.at[M + to], g_r.at[M + chip], there, s),
        )

    def maps(k, rows):
        own, other = aff[k, rows, :], px[lax.rem(k, H), rows, :]
        return jnp.where(core == 0, own, other), jnp.where(core == 0, other, own)

    def take(frm, part):
        ver[frm] = part
        aff[frm] = aff[frm] + part

        @pl.when(frm // H != core)
        def _():
            swap(frm).start()

    def e_take(k):
        frm = from_of(k)
        remote(eq.at[0], er_q.at[frm], e_s.at[frm], e_r.at[frm], t, frm).wait_recv()
        remote(eu.at[0], er_u.at[frm], e_s.at[frm], e_r.at[S + frm], t, frm).wait_recv()
        take(frm, decoded(er_q[frm], er_u[frm]))

    def composed(frm):
        @pl.when(frm // H == core)
        def _():
            swap(frm).wait_recv()
            speed = lines(rate, frm)
            for r in range(ratio):
                block = lax.rem(frm, H) * ratio + r
                lo, hi = maps(frm, slice(r * rb, r * rb + rb))
                steps, unit = coded(decay(high, speed[r * rb : r * rb + rb]) * lo + hi)
                gs_q[block] = steps
                gs_u[block] = jnp.concatenate(
                    [low[0:1] * high[0:1], low[1:2] + high[1:2], unit, unit], axis=0
                )

                @pl.when(block != chip)
                def _():
                    for c in g_copies(block):
                        c.start()

    take(s, solution_of(s))
    e_take(0)

    composed(s)

    def stream(k):
        e_take(k + 1)
        composed(from_of(k))

    loop(S - 2, stream)
    composed(from_of(S - 2))
    gr_q[chip] = gs_q[chip]
    gr_u[chip] = gs_u[chip]

    def plane(ref, z):
        return ref[:, pl.ds(pl.multiple_of(z * xb, xb), xb), :]

    def defect(z):
        rows = pl.ds(pl.multiple_of(z * xb, xb), xb)
        ver[:, rows, :] = ver[:, rows, :] - planar[z].reshape(S, xb, ny)

    loop(nz, defect)

    def cells(ref, block):
        k, r = core * H + block // ratio, lax.rem(block, ratio)
        return ref.at[pl.ds(r * zr, zr), pl.ds(pl.multiple_of(k * xb, xb), xb)]

    def i_copies(to):
        there = 2 * to + core
        return (
            remote(is_q.at[to], ir_q.at[chip], i_s.at[to], i_r.at[chip], there, s),
            remote(is_u.at[to], ir_u.at[chip], i_s.at[M + to], i_r.at[M + chip], there, s),
        )

    speed = cells(rate, chip)[...].reshape(rb, ny)

    def close(m, carry):
        total, kept, length = carry

        @pl.when(m != chip)
        def _():
            there = 2 * m + core
            remote(gs_q.at[0], gr_q.at[m], g_s.at[m], g_r.at[m], there, s).wait_recv()
            remote(gs_u.at[0], gr_u.at[m], g_s.at[m], g_r.at[M + m], there, s).wait_recv()

        h, d = gr_u[m, 0:1], gr_u[m, 1:2]
        factor = h * jnp.exp(-(speed * d))
        term = decoded(gr_q[m], gr_u[m, 2:3])
        jm[m] = factor
        gf[m] = term
        return factor * total + term, kept * h, length + d

    total, kept, length = lax.fori_loop(
        0, M, close,
        (jnp.zeros((rb, ny), F32), jnp.ones((1, ny), F32), jnp.zeros((1, ny), F32)),
    )

    def march(m, state):
        states[m] = state
        return jm[m] * state + gf[m]

    lax.fori_loop(0, M, march, total / (1.0 - kept * jnp.exp(-(speed * length))))

    def leave(k):
        to = lax.rem(chip + stride(k, M), M)
        is_q[to], is_u[to] = coded(states[to])
        for c in i_copies(to):
            c.start()

    loop(M - 1, leave)

    def give(block):
        return remote(
            cells(ps, block), cells(vb.at[pl.ds(1, nz)], block),
            give_s.at[block], give_r.at[block], mate, s,
        )

    def predict(block, p0):
        k, r = core * H + block // ratio, lax.rem(block, ratio)
        lo, _ = maps(k, pl.ds(pl.multiple_of(r * rb, rb), rb))
        p1 = decay(low, cells(rate, block)[...].reshape(rb, ny)) * p0 + lo
        mine = jnp.where(core == 0, p0, p1).reshape(zr, xb, ny)
        there = (pl.ds(r * zr, zr), pl.ds(pl.multiple_of(k * xb, xb), xb))
        here = (pl.ds(1 + r * zr, zr), pl.ds(pl.multiple_of(k * xb, xb), xb))
        vb[here] = mine
        q[here] = conductivity(mine)
        ps[there] = jnp.where(core == 0, p1, p0).reshape(zr, xb, ny)
        give(block).start()

    predict(chip, states[chip])

    def i_take(k):
        frm = lax.rem(chip + M - stride(k, M), M)
        there = 2 * frm + core
        remote(is_q.at[0], ir_q.at[frm], i_s.at[frm], i_r.at[frm], there, s).wait_recv()
        remote(is_u.at[0], ir_u.at[frm], i_s.at[frm], i_r.at[M + frm], there, s).wait_recv()
        predict(frm, decoded(ir_q[frm], ir_u[frm]))

    loop(M - 1, i_take)
    xs = pl.ds(pl.multiple_of(base_x, nx // 2), nx // 2)
    hb = []
    for i, (src, z, side, to) in enumerate(
        (
            (ps, 0, 1, down), (ps, nz - 1, 0, up), (vb, 1, 1, down), (vb, nz, 0, up),
        )
    ):
        hb.append(
            remote(
                src.at[z, xs], vb.at[side * (nz + 1), xs],
                hb_s.at[i], hb_r.at[2 * side + core], mate if i < 2 else t, to,
            )
        )
    for c in hb:
        c.start()

    def give_take(k):
        frm = lax.rem(chip + k, M)
        x = (1 - core) * H + frm // ratio
        where = (pl.ds(1 + lax.rem(frm, ratio) * zr, zr), pl.ds(pl.multiple_of(x * xb, xb), xb))
        remote(cells(ps, frm), vb.at[where], give_s.at[frm], give_r.at[frm], mate, s).wait_recv()
        q[where] = conductivity(vb[where])

    loop(M, give_take)

    def o_copies(z):
        return (
            remote(oq.at[z], out_q.at[z], o_s.at[z], o_r.at[z], nt, s),
            remote(ou.at[z], out_u.at[z], o_s.at[nz + z], o_r.at[nz + z], nt, s),
        )

    def second(i):
        @pl.when(i == nz // 2 - 1)
        def _():
            for side in range(2):
                for c in range(2):
                    remote(
                        ps.at[0, xs], vb.at[side * (nz + 1), pl.ds(c * (nx // 2), nx // 2)],
                        hb_s.at[0], hb_r.at[2 * side + c], t, down,
                    ).wait_recv()
            edges(vb)

        z0, z1 = pair(i)
        c0, p = solved(vb, z0)
        c1, r = solved(vb, z1)
        oq[z0], ou[z0] = coded(c0 + p + plane(ver, z0).reshape(nx, ny))
        oq[z1], ou[z1] = coded(c1 + r + plane(ver, z1).reshape(nx, ny))
        for c in o_copies(z0) + o_copies(z1):
            c.start()

    loop(nz // 2, second)

    def sent(copies):
        for c in copies:
            c.wait_send()

    sent(halo + [mates] + hb)
    loop(S - 1, lambda k: c_copy(k).wait_send())
    loop(S - 1, lambda k: sent(e_copies(lax.rem(s + 1 + k, S))))
    loop(H, lambda k: swap((1 - core) * H + k).wait_send())
    loop(M - 1, lambda k: sent(g_copies(lax.rem(chip + 1 + k, M))))
    loop(M - 1, lambda k: sent(i_copies(lax.rem(chip + 1 + k, M))))
    loop(M, lambda k: give(k).wait_send())

    def arrived(z):
        for c in o_copies(z):
            c.wait()

    loop(nz, arrived)


def per_device(T, S, starts, holes, rate, zones, htc, gas, hold, duration, inv_x, inv_y, inv_z):
    _, nz, nx, ny = starts.shape
    xb, M = nx // S, T // 2
    blk, rb = nz * xb, nz * nx // 2 // M
    hbm = pl.BlockSpec(memory_space=pltpu.HBM)
    smem = pl.BlockSpec(memory_space=pltpu.SMEM)
    dma = lambda n: pltpu.SemaphoreType.DMA((n,))
    i16 = lambda *shape: pltpu.VMEM(shape, jnp.int16)
    v32 = lambda *shape: pltpu.VMEM(shape, F32)
    steps, unit = pl.pallas_call(
        functools.partial(kernel, T, S),
        out_shape=(
            jax.ShapeDtypeStruct((nz, nx, ny), jnp.int16),
            jax.ShapeDtypeStruct((nz, 1, ny), F32),
        ),
        in_specs=[hbm, hbm, hbm, hbm, smem, smem, smem, smem, hbm, hbm, hbm],
        out_specs=(hbm, hbm),
        scratch_shapes=[
            v32(nz, nx, ny), pltpu.VMEM((nz, nx, ny), jnp.int32), v32(nz, nx, ny),
            pltpu.VMEM((2 * nz, nx), jnp.int32), pltpu.VMEM((nx, nx), BF16),
            pltpu.VMEM((ny, ny), BF16), pltpu.VMEM((S * nz, S * nz), BF16), dma(7),
            v32(nz + 2, nx, ny), v32(nz + 2, nx, ny), v32(nz + 2, nx, ny),
            pltpu.VMEM((ny, ny), BF16),
            v32(ny, nx), v32(nx, ny), v32(nx, ny),
            v32(8, ny), v32(8, ny),
            v32(nz, nx, ny), v32(nx * nz, ny),
            pltpu.VMEM((nx, nz, ny), BF16), pltpu.VMEM((S, xb, nz, ny), BF16),
            v32(S * blk, ny), v32(S, blk, ny), v32(S // 2, blk, ny),
            v32(S, blk, ny), v32(nz, nx, ny),
            v32(M, rb, ny), v32(M, rb, ny), v32(M, rb, ny),
            i16(S, blk, ny), v32(S, 1, ny), i16(S, blk, ny), v32(S, 1, ny),
            i16(M, rb, ny), v32(M, 4, ny), i16(M, rb, ny), v32(M, 4, ny),
            i16(M, rb, ny), v32(M, 1, ny), i16(M, rb, ny), v32(M, 1, ny),
            i16(nz, nx, ny), v32(nz, 1, ny),
            dma(2), dma(2), dma(1), dma(1), dma(S), dma(S), dma(2 * S), dma(2 * S),
            dma(S // 2), dma(S // 2),
            dma(2 * M), dma(2 * M), dma(2 * M), dma(2 * M), dma(M), dma(M), dma(4), dma(4),
            dma(2 * nz), dma(2 * nz),
        ],
        compiler_params=pltpu.CompilerParams(
            collective_id=0, has_side_effects=True, vmem_limit_bytes=60 * 1024 * 1024
        ),
    )(
        starts[0], holes, rate, zones.reshape(2 * nz, nx),
        htc, gas, hold, duration, inv_x, inv_y, inv_z,
    )
    return (steps.astype(F32) * unit)[None]


def solution(mesh):
    return jax.shard_map(
        functools.partial(per_device, mesh.shape["tm"], mesh.shape["space"]),
        mesh=mesh,
        in_specs=(
            P("tm", "space", None, None),
            P("space", None, None),
            P("space", None, None),
            P(None, "space", None),
            P(),
            P("tm", None),
            P("tm"),
            P("tm"),
            P(),
            P(),
            P(),
        ),
        out_specs=P("tm", "space", None, None),
        check_vma=False,
    )
```

```python
import functools

import jax
import jax.numpy as jnp
from jax import lax
from jax.experimental import pallas as pl
from jax.experimental.pallas import tpu as pltpu
from jax.sharding import PartitionSpec as P

COOLING = 4.0
COOLANT = -1.0
TIME_STEP = 0.2
MESH = pl.DeviceIdType.MESH
F32 = jnp.float32
BF16 = jnp.bfloat16


def loop(count, body):
    lax.fori_loop(0, count, lambda i, c: (body(i), c)[1], 0)


def kernel(
    T, S,
    u_in, holes_in, rate_in, zones_in, htc, gas, hold, duration, inv_x_in, inv_y_in, inv_z_in,
    out_q, out_u,
    u, holes, rate, zones, inv_x, inv_y, inv_z, load_s,
    va, vb, q, iyt, rows_tab, coef_tab, temp_tab, meta, meta_pt,
    planar, turned, cs, cr, es, aff, px, ver, ps, jm, gf, states, still, slope,
    eq, eu, er_q, er_u, gs_q, gs_u, gr_q, gr_u, is_q, is_u, ir_q, ir_u, oq, ou,
    halo_s, halo_r, meta_s, meta_r, c_s, c_r, e_s, e_r, swap_s, swap_r,
    g_s, g_r, i_s, i_r, give_s, give_r, hb_s, hb_r, o_s, o_r,
):
    t, s = lax.axis_index("tm"), lax.axis_index("space")
    core = lax.rem(t, 2)
    chip = t // 2
    M, H = T // 2, S // 2
    mate = t + 1 - 2 * core
    nt, pt = lax.rem(t + 1, T), lax.rem(t + T - 1, T)
    down, up = lax.rem(s + S - 1, S), lax.rem(s + 1, S)
    nz, nx, ny = u.shape
    xb = nx // S
    blk = nz * xb
    rb = nz * nx // 2 // M
    zr = rb // xb
    ratio = blk // rb
    base_x = core * (nx // 2)

    def remote(src, dst, send, recv, tt, ss):
        return pltpu.make_async_remote_copy(
            src_ref=src, dst_ref=dst, send_sem=send, recv_sem=recv,
            device_id=(tt, ss), device_id_type=MESH,
        )

    loads = [
        pltpu.make_async_copy(src, dst, load_s.at[i])
        for i, (src, dst) in enumerate(
            (
                (u_in, u), (zones_in, zones), (inv_y_in, inv_y), (inv_x_in, inv_x),
                (holes_in, holes), (rate_in, rate), (inv_z_in, inv_z),
            )
        )
    ]
    for c in loads:
        c.start()

    barrier = pltpu.get_barrier_semaphore()

    def greet(tt, ss):
        pl.semaphore_signal(barrier, inc=1, device_id=(tt, ss), device_id_type=MESH)

    loop(S - 1, lambda k: greet(t, lax.rem(s + 1 + k, S)))
    loop(M - 1, lambda k: greet(2 * lax.rem(chip + 1 + k, M) + core, s))
    greet(mate, s)
    greet(mate, down)
    greet(mate, up)
    greet(pt, s)
    loads[0].wait()
    pl.semaphore_wait(barrier, S - 1 + M - 1 + 4)

    halo = [
        remote(u.at[nz - 1], va.at[0], halo_s.at[0], halo_r.at[0], t, up),
        remote(u.at[0], va.at[nz + 1], halo_s.at[1], halo_r.at[1], t, down),
    ]
    for c in halo:
        c.start()
    meta[0:1, :] = jnp.full((1, ny), hold[0], F32)
    meta[1:2, :] = jnp.full((1, ny), duration[0] * (1.0 / T), F32)
    meta[2:8, :] = jnp.zeros((6, ny), F32)
    mates = remote(meta, meta_pt, meta_s.at[0], meta_r.at[0], mate, s)
    mates.start()

    for c in loads[1:]:
        c.wait()
    zid = zones[...]
    coef = jnp.zeros(zid.shape, F32)
    temp = jnp.zeros(zid.shape, F32)
    for k in range(htc.shape[0]):
        coef = jnp.where(zid == k, htc[k], coef)
        temp = jnp.where(zid == k, gas[0, k], temp)
    for tab, values in ((coef_tab, coef), (temp_tab, temp)):
        rows_tab[...] = jnp.zeros_like(rows_tab)
        for z in range(nz):
            rows_tab[2 * z : 2 * z + 1, :] = values[z : z + 1, :]
            at = (2 * z - 1) % ny
            rows_tab[at : at + 1, :] = values[nz + z : nz + z + 1, :]
        tab[...] = rows_tab[...].T
    iyt[...] = inv_y[...].astype(F32).T.astype(BF16)

    row = lax.broadcasted_iota(jnp.int32, (nx, ny), 0)
    lane = lax.broadcasted_iota(jnp.int32, (nx, ny), 1)

    def conductivity(v):
        return 0.5 + 0.25 * jnp.tanh(v)

    def edges(v):
        v[0] = jnp.where(s > 0, v[0], 0.0)
        v[nz + 1] = jnp.where(s < S - 1, v[nz + 1], 0.0)
        q[0] = conductivity(v[0])
        q[nz + 1] = conductivity(v[nz + 1])

    def at_faces(z):
        turn = lax.rem(ny - 2 * z, ny)
        on_face = (lane == 0) | (lane == ny - 1)
        face_coef = jnp.where(on_face, pltpu.roll(coef_tab[...], turn, 1), 0.0)
        return face_coef, pltpu.roll(temp_tab[...], turn, 1)

    def source_now(z, c):
        face_coef, face_temp = at_faces(z)
        cooled = COOLING * holes[z].astype(F32) * (COOLANT - c)
        return face_coef * (face_temp - c) + cooled

    def source_kept(z, c):
        return still[z] - slope[z] * c

    def solved(v, z, source):
        c, qc = v[z + 1], q[z + 1]
        outer = (qc + 0.5) * c
        flux = (q[z + 2] + qc) * (v[z + 2] - c) - (q[z] + qc) * (c - v[z])
        for axis, index, last in ((0, row, nx - 1), (1, lane, ny - 1)):
            n = c.shape[axis]
            vn, qn = pltpu.roll(c, n - 1, axis), pltpu.roll(qc, n - 1, axis)
            ahead = jnp.where(index == last, -outer, (qn + qc) * (vn - c))
            behind = jnp.where(index == 0, outer, pltpu.roll(ahead, 1, axis))
            flux = flux + ahead - behind
        e = (TIME_STEP * (flux + source(z, c))).astype(BF16)
        x = jnp.dot(inv_x[...], e, preferred_element_type=F32).astype(BF16)
        return c, jnp.dot(x, iyt[...], preferred_element_type=F32)

    def coded(v):
        top = jnp.max(jnp.abs(v), axis=0, keepdims=True)
        unit = jnp.maximum(top, 1e-30) * (1.0 / 32767.0)
        steps = jnp.round(v * (1.0 / unit))
        return steps.astype(jnp.int32).astype(jnp.int16), unit

    def decoded(steps, unit):
        return steps.astype(jnp.int32).astype(F32) * unit

    def own_copy(i):
        field = u[i]
        va[i + 1] = field
        q[i + 1] = conductivity(field)

    loop(nz, own_copy)

    def keep(z, p):
        planar[z] = p
        turned[pl.ds(z, nx, stride=nz), :] = p

    def pair(i):
        return 1 + 2 * i, lax.rem(2 + 2 * i, nz)

    def first(i):
        @pl.when(i == nz // 2 - 1)
        def _():
            halo[0].wait_recv()
            halo[1].wait_recv()
            edges(va)

        z0, z1 = pair(i)
        _, p = solved(va, z0, source_now)
        _, r = solved(va, z1, source_now)
        keep(z0, p)
        keep(z1, r)

    loop(nz // 2, first)

    def stride(k, size=S):
        odd = lax.rem(k, 2)
        return (1 - odd) * (1 + k // 2) + odd * (size - 1 - k // 2)

    def to_of(k):
        return lax.rem(s + stride(k), S)

    def from_of(k):
        return lax.rem(s + S - stride(k), S)

    def c_copy(k):
        to = to_of(k)
        return remote(
            cs.at[pl.ds(to * xb, xb)], cr.at[s], c_s.at[to], c_r.at[s], t, to
        )

    def c_block(to):
        block = turned[pl.ds(to * blk, blk), :]
        return block.reshape(xb, nz, ny).astype(BF16)

    def c_send(k):
        to = to_of(k)
        cs[pl.ds(to * xb, xb)] = c_block(to)
        c_copy(k).start()

    loop(S - 1, c_send)
    cr[s] = c_block(s)

    def decay(m, speed):
        return m[0:1, :] * jnp.exp(-(speed * m[1:2, :]))

    def lines(ref, k):
        return ref[:, pl.ds(pl.multiple_of(k * xb, xb), xb), :].reshape(blk, ny)

    def base(k):
        field = lines(u, k)
        aff[k] = field - decay(meta, lines(rate, k)) * field

    loop(S, base)

    def keep_source(z):
        face_coef, face_temp = at_faces(z)
        hole = COOLING * holes[z].astype(F32)
        still[z] = face_coef * face_temp + COOLANT * hole
        slope[z] = face_coef + hole

    loop(nz, keep_source)
    mates.wait_recv()
    low = jnp.where(core == 0, meta[...], meta_pt[...])
    high = jnp.where(core == 0, meta_pt[...], meta[...])

    def c_wait(k):
        frm = lax.rem(s + 1 + k, S)
        remote(cs.at[pl.ds(0, xb)], cr.at[frm], c_s.at[frm], c_r.at[frm], t, frm).wait_recv()

    loop(S - 1, c_wait)
    def solve(x):
        es[pl.ds(x, S * nz, stride=xb), :] = jnp.dot(
            inv_z[...], cr[:, x].reshape(S * nz, ny), preferred_element_type=F32
        )

    loop(xb, solve)

    def solution_of(k):
        return es[pl.ds(pl.multiple_of(k * blk, blk), blk), :]

    def e_copies(to):
        return (
            remote(eq.at[to], er_q.at[s], e_s.at[to], e_r.at[s], t, to),
            remote(eu.at[to], er_u.at[s], e_s.at[S + to], e_r.at[S + s], t, to),
        )

    def e_send(k):
        to = to_of(k)
        eq[to], eu[to] = coded(solution_of(to))
        for c in e_copies(to):
            c.start()

    loop(S - 1, e_send)

    def swap(k):
        return remote(
            aff.at[k], px.at[lax.rem(k, H)],
            swap_s.at[lax.rem(k, H)], swap_r.at[lax.rem(k, H)], mate, s,
        )

    def g_copies(to):
        there = 2 * to + core
        return (
            remote(gs_q.at[to], gr_q.at[chip], g_s.at[to], g_r.at[chip], there, s),
            remote(gs_u.at[to], gr_u.at[chip], g_s.at[M + to], g_r.at[M + chip], there, s),
        )

    def maps(k, rows):
        own, other = aff[k, rows, :], px[lax.rem(k, H), rows, :]
        return jnp.where(core == 0, own, other), jnp.where(core == 0, other, own)

    def take(frm, part):
        ver[frm] = part
        aff[frm] = aff[frm] + part

        @pl.when(frm // H != core)
        def _():
            swap(frm).start()

    def e_take(k):
        frm = from_of(k)
        remote(eq.at[0], er_q.at[frm], e_s.at[frm], e_r.at[frm], t, frm).wait_recv()
        remote(eu.at[0], er_u.at[frm], e_s.at[frm], e_r.at[S + frm], t, frm).wait_recv()
        take(frm, decoded(er_q[frm], er_u[frm]))

    def composed(frm):
        @pl.when(frm // H == core)
        def _():
            swap(frm).wait_recv()
            speed = lines(rate, frm)
            for r in range(ratio):
                block = lax.rem(frm, H) * ratio + r
                lo, hi = maps(frm, slice(r * rb, r * rb + rb))
                steps, unit = coded(decay(high, speed[r * rb : r * rb + rb]) * lo + hi)
                gs_q[block] = steps
                gs_u[block] = jnp.concatenate(
                    [low[0:1] * high[0:1], low[1:2] + high[1:2], unit, unit], axis=0
                )

                @pl.when(block != chip)
                def _():
                    for c in g_copies(block):
                        c.start()

    take(s, solution_of(s))
    e_take(0)

    composed(s)

    def stream(k):
        e_take(k + 1)
        composed(from_of(k))

    loop(S - 2, stream)
    composed(from_of(S - 2))
    gr_q[chip] = gs_q[chip]
    gr_u[chip] = gs_u[chip]

    def plane(ref, z):
        return ref[:, pl.ds(pl.multiple_of(z * xb, xb), xb), :]

    def defect(z):
        rows = pl.ds(pl.multiple_of(z * xb, xb), xb)
        ver[:, rows, :] = ver[:, rows, :] - planar[z].reshape(S, xb, ny)

    loop(nz, defect)

    def cells(ref, block):
        k, r = core * H + block // ratio, lax.rem(block, ratio)
        return ref.at[pl.ds(r * zr, zr), pl.ds(pl.multiple_of(k * xb, xb), xb)]

    def i_copies(to):
        there = 2 * to + core
        return (
            remote(is_q.at[to], ir_q.at[chip], i_s.at[to], i_r.at[chip], there, s),
            remote(is_u.at[to], ir_u.at[chip], i_s.at[M + to], i_r.at[M + chip], there, s),
        )

    speed = cells(rate, chip)[...].reshape(rb, ny)

    def close(m, carry):
        total, kept, length = carry

        @pl.when(m != chip)
        def _():
            there = 2 * m + core
            remote(gs_q.at[0], gr_q.at[m], g_s.at[m], g_r.at[m], there, s).wait_recv()
            remote(gs_u.at[0], gr_u.at[m], g_s.at[m], g_r.at[M + m], there, s).wait_recv()

        h, d = gr_u[m, 0:1], gr_u[m, 1:2]
        factor = h * jnp.exp(-(speed * d))
        term = decoded(gr_q[m], gr_u[m, 2:3])
        jm[m] = factor
        gf[m] = term
        return factor * total + term, kept * h, length + d

    total, kept, length = lax.fori_loop(
        0, M, close,
        (jnp.zeros((rb, ny), F32), jnp.ones((1, ny), F32), jnp.zeros((1, ny), F32)),
    )

    def march(m, state):
        states[m] = state
        return jm[m] * state + gf[m]

    lax.fori_loop(0, M, march, total / (1.0 - kept * jnp.exp(-(speed * length))))

    def leave(k):
        to = lax.rem(chip + stride(k, M), M)
        is_q[to], is_u[to] = coded(states[to])
        for c in i_copies(to):
            c.start()

    loop(M - 1, leave)

    def give(block):
        return remote(
            cells(ps, block), cells(vb.at[pl.ds(1, nz)], block),
            give_s.at[block], give_r.at[block], mate, s,
        )

    def predict(block, p0):
        k, r = core * H + block // ratio, lax.rem(block, ratio)
        lo, _ = maps(k, pl.ds(pl.multiple_of(r * rb, rb), rb))
        p1 = decay(low, cells(rate, block)[...].reshape(rb, ny)) * p0 + lo
        mine = jnp.where(core == 0, p0, p1).reshape(zr, xb, ny)
        there = (pl.ds(r * zr, zr), pl.ds(pl.multiple_of(k * xb, xb), xb))
        here = (pl.ds(1 + r * zr, zr), pl.ds(pl.multiple_of(k * xb, xb), xb))
        vb[here] = mine
        q[here] = conductivity(mine)
        ps[there] = jnp.where(core == 0, p1, p0).reshape(zr, xb, ny)
        give(block).start()

    predict(chip, states[chip])

    def i_take(k):
        frm = lax.rem(chip + M - stride(k, M), M)
        there = 2 * frm + core
        remote(is_q.at[0], ir_q.at[frm], i_s.at[frm], i_r.at[frm], there, s).wait_recv()
        remote(is_u.at[0], ir_u.at[frm], i_s.at[frm], i_r.at[M + frm], there, s).wait_recv()
        predict(frm, decoded(ir_q[frm], ir_u[frm]))

    loop(M - 1, i_take)
    xs = pl.ds(pl.multiple_of(base_x, nx // 2), nx // 2)
    hb = []
    for i, (src, z, side, to) in enumerate(
        (
            (ps, 0, 1, down), (ps, nz - 1, 0, up), (vb, 1, 1, down), (vb, nz, 0, up),
        )
    ):
        hb.append(
            remote(
                src.at[z, xs], vb.at[side * (nz + 1), xs],
                hb_s.at[i], hb_r.at[2 * side + core], mate if i < 2 else t, to,
            )
        )
    for c in hb:
        c.start()

    def give_take(k):
        frm = lax.rem(chip + k, M)
        x = (1 - core) * H + frm // ratio
        where = (pl.ds(1 + lax.rem(frm, ratio) * zr, zr), pl.ds(pl.multiple_of(x * xb, xb), xb))
        remote(cells(ps, frm), vb.at[where], give_s.at[frm], give_r.at[frm], mate, s).wait_recv()
        q[where] = conductivity(vb[where])

    loop(M, give_take)

    def o_copies(z):
        return (
            remote(oq.at[z], out_q.at[z], o_s.at[z], o_r.at[z], nt, s),
            remote(ou.at[z], out_u.at[z], o_s.at[nz + z], o_r.at[nz + z], nt, s),
        )

    def second(i):
        @pl.when(i == nz // 2 - 1)
        def _():
            for side in range(2):
                for c in range(2):
                    remote(
                        ps.at[0, xs], vb.at[side * (nz + 1), pl.ds(c * (nx // 2), nx // 2)],
                        hb_s.at[0], hb_r.at[2 * side + c], t, down,
                    ).wait_recv()
            edges(vb)

        z0, z1 = pair(i)
        c0, p = solved(vb, z0, source_kept)
        c1, r = solved(vb, z1, source_kept)
        oq[z0], ou[z0] = coded(c0 + p + plane(ver, z0).reshape(nx, ny))
        oq[z1], ou[z1] = coded(c1 + r + plane(ver, z1).reshape(nx, ny))
        for c in o_copies(z0) + o_copies(z1):
            c.start()

    loop(nz // 2, second)

    def sent(copies):
        for c in copies:
            c.wait_send()

    sent(halo + [mates] + hb)
    loop(S - 1, lambda k: c_copy(k).wait_send())
    loop(S - 1, lambda k: sent(e_copies(lax.rem(s + 1 + k, S))))
    loop(H, lambda k: swap((1 - core) * H + k).wait_send())
    loop(M - 1, lambda k: sent(g_copies(lax.rem(chip + 1 + k, M))))
    loop(M - 1, lambda k: sent(i_copies(lax.rem(chip + 1 + k, M))))
    loop(M, lambda k: give(k).wait_send())

    def arrived(z):
        for c in o_copies(z):
            c.wait()

    loop(nz, arrived)


def per_device(T, S, starts, holes, rate, zones, htc, gas, hold, duration, inv_x, inv_y, inv_z):
    _, nz, nx, ny = starts.shape
    xb, M = nx // S, T // 2
    blk, rb = nz * xb, nz * nx // 2 // M
    hbm = pl.BlockSpec(memory_space=pltpu.HBM)
    smem = pl.BlockSpec(memory_space=pltpu.SMEM)
    dma = lambda n: pltpu.SemaphoreType.DMA((n,))
    i16 = lambda *shape: pltpu.VMEM(shape, jnp.int16)
    v32 = lambda *shape: pltpu.VMEM(shape, F32)
    steps, unit = pl.pallas_call(
        functools.partial(kernel, T, S),
        out_shape=(
            jax.ShapeDtypeStruct((nz, nx, ny), jnp.int16),
            jax.ShapeDtypeStruct((nz, 1, ny), F32),
        ),
        in_specs=[hbm, hbm, hbm, hbm, smem, smem, smem, smem, hbm, hbm, hbm],
        out_specs=(hbm, hbm),
        scratch_shapes=[
            v32(nz, nx, ny), pltpu.VMEM((nz, nx, ny), jnp.int32), v32(nz, nx, ny),
            pltpu.VMEM((2 * nz, nx), jnp.int32), pltpu.VMEM((nx, nx), BF16),
            pltpu.VMEM((ny, ny), BF16), pltpu.VMEM((S * nz, S * nz), BF16), dma(7),
            v32(nz + 2, nx, ny), v32(nz + 2, nx, ny), v32(nz + 2, nx, ny),
            pltpu.VMEM((ny, ny), BF16),
            v32(ny, nx), v32(nx, ny), v32(nx, ny),
            v32(8, ny), v32(8, ny),
            v32(nz, nx, ny), v32(nx * nz, ny),
            pltpu.VMEM((nx, nz, ny), BF16), pltpu.VMEM((S, xb, nz, ny), BF16),
            v32(S * blk, ny), v32(S, blk, ny), v32(S // 2, blk, ny),
            v32(S, blk, ny), v32(nz, nx, ny),
            v32(M, rb, ny), v32(M, rb, ny), v32(M, rb, ny),
            v32(nz, nx, ny), v32(nz, nx, ny),
            i16(S, blk, ny), v32(S, 1, ny), i16(S, blk, ny), v32(S, 1, ny),
            i16(M, rb, ny), v32(M, 4, ny), i16(M, rb, ny), v32(M, 4, ny),
            i16(M, rb, ny), v32(M, 1, ny), i16(M, rb, ny), v32(M, 1, ny),
            i16(nz, nx, ny), v32(nz, 1, ny),
            dma(2), dma(2), dma(1), dma(1), dma(S), dma(S), dma(2 * S), dma(2 * S),
            dma(S // 2), dma(S // 2),
            dma(2 * M), dma(2 * M), dma(2 * M), dma(2 * M), dma(M), dma(M), dma(4), dma(4),
            dma(2 * nz), dma(2 * nz),
        ],
        compiler_params=pltpu.CompilerParams(
            collective_id=0, has_side_effects=True, vmem_limit_bytes=60 * 1024 * 1024
        ),
    )(
        starts[0], holes, rate, zones.reshape(2 * nz, nx),
        htc, gas, hold, duration, inv_x, inv_y, inv_z,
    )
    return (steps.astype(F32) * unit)[None]


def solution(mesh):
    return jax.shard_map(
        functools.partial(per_device, mesh.shape["tm"], mesh.shape["space"]),
        mesh=mesh,
        in_specs=(
            P("tm", "space", None, None),
            P("space", None, None),
            P("space", None, None),
            P(None, "space", None),
            P(),
            P("tm", None),
            P("tm"),
            P("tm"),
            P(),
            P(),
            P(),
        ),
        out_specs=P("tm", "space", None, None),
        check_vma=False,
    )
```
